32 devices in a mesh: seg: 4 (over y, x), blk: 8 (over z, core).
Axes of the slice: x: 2, y: 2, z: 4, core: 2. Of those that a mesh axis runs over, the one named last changes fastest.
Arguments:
- queries: bfloat16 [1024, 2048], P('blk'), may hold values from -8 to 8
- new_kv: bfloat16 [1024, 256], P('blk'), may hold values from -8 to 8
- cache_kv: bfloat16 [16384, 256], P(('seg', 'blk')), may hold values from -8 to 8
- cache_len: int32 [32], replicated, may hold values from 256 to 384
- page_owner: int32 [128, 1], replicated, may hold values from 0 to 31; in each aligned block of 128 rows (0 to 127, 128 to 255, ...) at most 16 rows name the same one
Outputs:
- attn_out: bfloat16 [1024, 2048], P('blk', 'seg')
- cache_out: bfloat16 [16384, 256], P(('seg', 'blk'))
The draws below stay inside these ranges and needn't reach their ends.
Inputs may be any that keep to these rules, and one draw needn't show every extreme that they name: `page_owner`: every device owns at least one page, no device owns more than 16 pages, and some device owns exactly 16.
All inputs are finite; a program needn't handle non-finite values.
Results may differ from the reference program's by a relative error of at most 0.018.
Values may be sent and summed in bfloat16 or wider, within the bound.
A program may use at most 64 MiB of HBM per device.

```python
import math
import jax
import jax.numpy as jnp
import numpy as np
from jax import lax

HQ = 16
HD = 128
SLOTS = 512
PAGE = 8
STRETCH = 1024
PAGES = 128
MAXP = 16
CACHE_ROWS = 16384
N_SEG = 4
N_BLK = 8


def sign_pattern(key):
    sign_bits = jax.random.bernoulli(key, 0.5, (HD,))
    return jnp.where(sign_bits, 1.0, -1.0).astype(jnp.float32)


def plant_queries(drawn, signs, strengths):
    row_index = jnp.arange(STRETCH)[:, None]
    col_index = jnp.arange(HQ * HD)[None, :]
    head_index = col_index // HD
    for member in range(8):
        token_row = member * STRETCH // 8 + STRETCH // 16
        aligned = (row_index == token_row) & (head_index == 3 * member % HQ)
        drawn = jnp.where(aligned, strengths[member] * signs[col_index % HD], drawn)
    return drawn


def plant_keys(key_rows, signs, strengths, lowered):
    row_index = jnp.arange(CACHE_ROWS)[:, None]
    lane_index = jnp.arange(HD)[None, :]
    for member in range(4):
        first_row = member * CACHE_ROWS // 4 + SLOTS // 4
        strong = strengths[member] * signs[None, :]
        second = jnp.where(lane_index == 0, (strengths[member] - lowered) * signs[None, :], strong)
        key_rows = jnp.where(row_index == first_row, strong, key_rows)
        key_rows = jnp.where(row_index == first_row + 1, second, key_rows)
    return key_rows


def draw_queries(key, part):
    signs = sign_pattern(key)
    key = jax.random.fold_in(key, 11)
    drawn = jnp.clip(2.0 * jax.random.normal(key, (STRETCH, HQ * HD), jnp.float32), -8.0, 8.0)
    return plant_queries(drawn, signs, [2.5, 2.5, 2.5, 2.5, 2.5, 2.5, 2.5, 2.5]).astype(jnp.bfloat16)


def draw_cache_kv(key, part):
    signs = sign_pattern(key)
    key = jax.random.fold_in(key, 23)
    key_part, value_part, scale_part = jax.random.split(key, 3)
    value_scale = jnp.exp(jax.random.uniform(scale_part, (CACHE_ROWS, 1), jnp.float32, math.log(0.3), math.log(3.0)))
    key_rows = jnp.clip(1.5 * jax.random.normal(key_part, (CACHE_ROWS, HD), jnp.float32), -8.0, 8.0)
    value_rows = jnp.clip(jax.random.normal(value_part, (CACHE_ROWS, HD), jnp.float32), -8.0, 8.0)
    key_rows = plant_keys(key_rows, signs, [8.0, 5.0, 8.0, 6.0], 9.0)
    return jnp.concatenate([key_rows, jnp.clip(value_rows * value_scale, -8.0, 8.0)], axis=1).astype(jnp.bfloat16)


def with_ends(values, key, least, largest):
    longest = values.shape.index(max(values.shape))
    spots = []
    for shift in (0, 1):
        where = [jax.random.randint(jax.random.fold_in(key, axis), (), 0, length) for axis, length in enumerate(values.shape)]
        where[longest] = (where[longest] + shift) % values.shape[longest]
        spots.append(tuple(where))
    return values.at[spots[0]].set(least).at[spots[1]].set(largest)


def shard_levels(stream_key, extent, shards, smallest, high):
    def one(dim, shards_of):
        heights = jax.random.uniform(jax.random.fold_in(jax.random.fold_in(stream_key, 6), dim), (shards_of,), jnp.float32, smallest / len(shards), high / len(shards))
        return jnp.repeat(jnp.exp(heights), extent[dim] // shards_of).reshape((-1,) + (1,) * (len(extent) - dim - 1))

    gain = one(*shards[0])
    for cut in shards[1:]:
        gain = gain * one(*cut)
    return gain


def assign_block(own_key, own, number, rows, count, top, most, slope):
    order = jax.random.permutation(own_key, count)
    crowded, common = portions_of(count, rows * top, most, slope, True), portions_of(count, rows * top, most, slope, False)
    places = jnp.arange(count)

    def named(tallies, turn):
        used = int((tallies > 0).sum())
        fixed = max(1, used // 4)
        passed = fixed + (places - fixed + turn * (used - fixed)) % max(1, count - fixed)
        return jnp.zeros((count,), jnp.int32).at[order[jnp.where(places < fixed, places, passed)]].set(jnp.asarray(tallies, jnp.int32))

    tallies = jnp.where(number % 4 == 0, named(crowded, number // 4), named(common, number - number // 4 - 1))
    mixed = jax.random.permutation(jax.random.fold_in(own, 3), count)
    donor, taker = mixed[0:count // 2 * 2:2], mixed[1:count // 2 * 2:2]
    room = jnp.minimum(tallies[donor] - 1, most - tallies[taker]) // 2
    room = jnp.where((donor == order[0]) | (taker == order[0]) | (tallies[taker] == 0), 0, jnp.maximum(room, 0))
    passed = jax.random.randint(jax.random.fold_in(own, 4), (count // 2,), 0, 1 << 20) % (room + 1)
    tallies = tallies.at[donor].add(-passed).at[taker].add(passed)
    labels = jnp.searchsorted(jnp.cumsum(tallies), jnp.arange(rows * top), side="right").astype(jnp.int32)
    table = labels.reshape(top, rows).T
    table = table[jax.random.permutation(jax.random.fold_in(own, 1), rows)]
    turn = jax.random.randint(jax.random.fold_in(own, 2), (rows, 1), 0, top)
    return jnp.take_along_axis(table, (jnp.arange(top)[None, :] + turn) % top, axis=1)


def portions_of(count, total, most, lean, full):
    loads = [(1 << 20) // math.isqrt(rank ** lean) + 1 for rank in range(1, count + 1)]
    largest = most if full else min(most, max(-(-total // count), total * loads[0] // sum(loads)))
    least = 1 if total - largest >= count - 1 else 0
    counts, spare = [largest] + [least] * (count - 1), total - largest - least * (count - 1)
    while spare > 0:
        free = [i for i in range(1, count) if counts[i] < largest] or [i for i in range(1, count) if counts[i] < most]
        pool, remaining = sum([loads[i] for i in free]), spare
        for i in free:
            more = min(most - counts[i], max(1, remaining * loads[i] // pool), spare)
            counts[i] = counts[i] + more
            spare = spare - more
    return np.array(counts)


def centred(key, dims, spread, limit, cuts=(), kind=jnp.bfloat16):
    gain = shard_levels(key, dims, cuts, -0.22, 0.18) if cuts else 1.0
    values = jax.random.normal(key, dims, jnp.float32) * spread * gain
    return jnp.minimum(jnp.maximum(values, -limit), limit).astype(kind)


def setup_inputs(seed: int = 0) -> dict:
    keys = jax.random.split(jax.random.key(seed), 6)
    queries = draw_queries(jax.random.fold_in(keys[5], 71), 0)
    new_kv = centred(keys[1], (STRETCH, 2 * HD), 1.5, 8.0, ((0, 8),))
    cache_kv = draw_cache_kv(jax.random.fold_in(keys[5], 71), 0)
    cache_len = with_ends(jax.random.randint(keys[3], (N_SEG * N_BLK,), SLOTS // 2, SLOTS - PAGE * MAXP + 1), jax.random.fold_in(keys[3], 1), SLOTS // 2, SLOTS - PAGE * MAXP).astype(jnp.int32)
    page_owner_keys = jax.random.split(jax.random.fold_in(keys[4], 1), PAGES // PAGES)
    page_owner_turns = jax.random.permutation(jax.random.fold_in(keys[4], 3), PAGES // PAGES)
    page_owner = jax.vmap(lambda own, number: assign_block(jax.random.fold_in(keys[4], 2), own, number, PAGES, N_SEG * N_BLK, 1, MAXP, 2))(page_owner_keys, page_owner_turns).reshape((PAGES, 1))
    return dict(queries=queries, new_kv=new_kv, cache_kv=cache_kv, cache_len=cache_len, page_owner=page_owner)


neg_large = -1e+30

def slot_table(device, cache_len, page_owner, slot_count, page_rows, span_rows):
    owners = page_owner[:, 0]
    page_total = owners.shape[0]
    owned_mask = (owners == device).astype(jnp.int32)
    earlier = jnp.cumsum(owned_mask) - owned_mask
    owned_count = jnp.sum(owned_mask)
    filled = cache_len[device]
    slot_ids = jnp.arange(slot_count, dtype=jnp.int32)
    offset = slot_ids - filled
    is_new = (offset >= 0) & (offset < page_rows * owned_count)
    wanted = offset // page_rows
    page_match = (owned_mask[None, :] == 1) & (earlier[None, :] == wanted[:, None])
    page_ids = jnp.arange(page_total, dtype=jnp.int32)
    page_of = lax.optimization_barrier(jnp.sum(jnp.where(page_match, page_ids[None, :], 0), axis=1))
    source_row = jnp.where(is_new, page_of * page_rows + offset % page_rows, 0).astype(jnp.int32)
    key_pos = jnp.where(slot_ids < filled, -1, jnp.where(is_new, source_row, span_rows)).astype(jnp.int32)
    return (source_row, key_pos, is_new)

def combine_parts(left, right):
    top_max = jnp.maximum(left[1], right[1])
    left_weight = jnp.exp(left[1] - top_max)
    right_weight = jnp.exp(right[1] - top_max)
    return (left[0] * left_weight[:, None] + right[0] * right_weight[:, None], top_max, left[2] * left_weight + right[2] * right_weight)

def reference(queries, new_kv, cache_kv, cache_len, page_owner):
    device_total = N_SEG * N_BLK
    caches = cache_kv.reshape(device_total, SLOTS, 2 * HD)

    def write(item):
        device, cache = item
        source_row, key_pos, is_new = slot_table(device, cache_len, page_owner, SLOTS, PAGE, STRETCH)
        return (jnp.where(is_new[:, None], jnp.take(new_kv, source_row, axis=0), cache), key_pos)
    new_caches, positions = lax.map(write, (jnp.arange(device_total, dtype=jnp.int32), caches))
    rows_q = queries.reshape(STRETCH * HQ, HD)
    q_pos = jnp.arange(STRETCH * HQ, dtype=jnp.int32) // HQ
    score_scale = 1.0 / math.sqrt(HD)

    def visit(carried, item):
        cache, key_pos = item
        key_rows = cache[:, :HD]
        value_rows = cache[:, HD:]
        scores = jnp.dot(rows_q, key_rows.T, preferred_element_type=jnp.float32) * score_scale
        visible = key_pos[None, :] <= q_pos[:, None]
        local_max = lax.optimization_barrier(jnp.max(jnp.where(visible, scores, neg_large), axis=1))
        weights = jnp.where(visible, jnp.exp(scores - local_max[:, None]), 0.0)
        local_sum = lax.optimization_barrier(jnp.sum(weights, axis=1))
        local_out = jnp.dot(weights.astype(jnp.bfloat16), value_rows, preferred_element_type=jnp.float32)
        return (combine_parts(carried, (local_out, local_max, local_sum)), None)
    start = (jnp.zeros((STRETCH * HQ, HD), jnp.float32), jnp.full((STRETCH * HQ,), neg_large, jnp.float32), jnp.zeros((STRETCH * HQ,), jnp.float32))
    (out_acc, row_max, row_sum), _ = lax.scan(visit, start, (new_caches, positions))
    attended = (out_acc / row_sum[:, None]).reshape(STRETCH, HQ * HD).astype(jnp.bfloat16)
    return (attended, new_caches.reshape(device_total * SLOTS, 2 * HD))
```

```python
import functools
import math

import jax
import jax.numpy as jnp
from jax import lax
from jax.experimental import pallas as pl
from jax.experimental.pallas import tpu as pltpu
from jax.sharding import PartitionSpec as P

PAGE = 8
HD = 128
NEG = -1e30
MESH = pl.DeviceIdType.MESH


def body(ns, nb, cap, low, tile, len_ref, q_ref, new_ref, cache_ref, owner_ref, attn_ref, cout_ref,
         held, news, q_s, m_s, acc_s, osend, lsend, orecv, lrecv,
         send_c, recv_c, send_n, recv_n, send_x, recv_x, send_o, recv_o, send_l, recv_l):
    s = lax.axis_index("seg")
    b = lax.axis_index("blk")
    nc = nb // 2
    z = b // 2
    core = b % 2
    sib = z * 2 + 1 - core
    me = s * nb + b
    toks = q_ref.shape[0]
    heads = q_ref.shape[1] // HD
    hpd = heads // ns
    rows_t = hpd * toks
    part = toks // ns
    slots = cache_ref.shape[0]
    scale = math.log2(math.e) / math.sqrt(HD)

    def shard(chip, c):
        return held.at[chip, pl.ds(pl.multiple_of(c * cap, 16), cap)]

    barrier = pltpu.get_barrier_semaphore()
    for d in range(1, nb):
        pl.semaphore_signal(barrier, inc=1, device_id=(s, (b + d) % nb), device_id_type=MESH)
    for d in range(1, ns):
        pl.semaphore_signal(barrier, inc=1, device_id=((s + d) % ns, b), device_id_type=MESH)
    held[z, pl.ds(pl.multiple_of(core * cap, 16), cap), :] = cache_ref[0:cap, :]
    news[s, b, :, :] = new_ref[pl.ds(pl.multiple_of(s * part, 16), part), :]
    pl.semaphore_wait(barrier, nb + ns - 2)

    def copy_c(chip, c, way, target):
        return pltpu.make_async_remote_copy(
            src_ref=shard(chip, c), dst_ref=shard(chip, c),
            send_sem=send_c.at[chip, way], recv_sem=recv_c.at[chip, c],
            device_id=(s, target), device_id_type=MESH)

    def copy_n(d):
        return pltpu.make_async_remote_copy(
            src_ref=news.at[s, b], dst_ref=news.at[s, b],
            send_sem=send_n.at[d], recv_sem=recv_n.at[b],
            device_id=(s, (b + d) % nb), device_id_type=MESH)

    def copy_x(d):
        return pltpu.make_async_remote_copy(
            src_ref=news.at[s], dst_ref=news.at[s],
            send_sem=send_x.at[d], recv_sem=recv_x.at[s],
            device_id=((s + d) % ns, b), device_id_type=MESH)

    copy_c(z, core, 2, sib).start()

    @pl.when(z > 0)
    def _():
        copy_c(z, core, 0, b - 2).start()

    @pl.when(z < nc - 1)
    def _():
        copy_c(z, core, 1, b + 2).start()

    for d in range(1, nb):
        copy_n(d).start()

    for h in range(heads):
        q_s[h * toks:(h + 1) * toks, :] = q_ref[:, h * HD:(h + 1) * HD]
    m_s[...] = jnp.full_like(m_s, NEG)
    acc_s[...] = jnp.zeros_like(acc_s)

    def online(row, keys, vals, valid):
        rows = pl.ds(pl.multiple_of(row, tile), tile)
        n = keys.shape[0]
        sc = lax.dot_general(q_s[rows, :], keys, (((1,), (1,)), ((), ())),
                             preferred_element_type=jnp.float32)
        parts = []
        for g in range(n // 128):
            piece = sc[:, g * 128:(g + 1) * 128]
            mask = valid(g)
            parts.append(piece if mask is None else jnp.where(mask, piece, NEG))
        top = functools.reduce(jnp.maximum, parts)
        old = m_s[rows, :]
        new = jnp.maximum(old, jnp.max(top, axis=1, keepdims=True))
        p = jnp.concatenate(
            [jnp.exp2((piece - new) * scale).astype(jnp.bfloat16) for piece in parts], axis=1)
        fix = jnp.exp2((old - new) * scale)
        vaug = jnp.concatenate([vals, jnp.ones_like(vals)], axis=1)
        pv = jnp.dot(p, vaug, preferred_element_type=jnp.float32)
        m_s[rows, :] = new
        acc_s[rows, 0:HD] = acc_s[rows, 0:HD] * fix + pv[:, 0:HD]
        acc_s[rows, HD:] = acc_s[rows, HD:] * fix + pv[:, HD:]

    def pair(chip, row):
        len0 = len_ref[s * nb + chip * 2]
        len1 = len_ref[s * nb + chip * 2 + 1]

        def valid(g):
            lo, hi = g * 128, g * 128 + 128
            if all(c % cap < low for c in range(lo, hi)):
                return None
            col = lo + lax.broadcasted_iota(jnp.int32, (1, 128), 1)
            return col < jnp.where(col < cap, len0, cap + len1)

        online(row, held[chip, :, 0:HD], held[chip, :, HD:], valid)

    def pair_all(chip):
        @pl.loop(0, ns)
        def _(j):
            for u in range(rows_t // tile):
                pair(chip, j * rows_t + u * tile)

    def new_all():
        def mask_for(g):
            col = g * 128 + lax.broadcasted_iota(jnp.int32, (1, 128), 1)
            pos = (col // part) * toks + s * part + col % part
            tok = b * toks + lax.broadcasted_iota(jnp.int32, (tile, 1), 0) % toks
            return pos <= tok

        @pl.loop(0, ns)
        def _(j):
            rows = news[s].reshape(nb * part, 2 * HD)
            for u in range(rows_t // tile):
                online(j * rows_t + u * tile, rows[:, 0:HD], rows[:, HD:], mask_for)

    def nth_chip(i):
        short = jnp.minimum(z, nc - 1 - z)
        far = i - short
        both = jnp.where(i % 2 == 1, z - (i + 1) // 2, z + (i + 1) // 2)
        single = jnp.where(2 * z < nc, z + far, z - far)
        return jnp.where(i <= 2 * short, both, single)

    def arrive(k):
        @pl.when(z - k >= 0)
        def _():
            copy_c(z - k, core, 1, b).wait_recv()

            @pl.when(z < nc - 1)
            def _():
                copy_c(z - k, core, 1, b + 2).start()
            copy_c(z - k, core, 2, sib).start()

        @pl.when(z + k < nc)
        def _():
            copy_c(z + k, core, 0, b).wait_recv()

            @pl.when(z > 0)
            def _():
                copy_c(z + k, core, 0, b - 2).start()
            copy_c(z + k, core, 2, sib).start()

    copy_c(z, 1 - core, 2, sib).wait_recv()
    pair_all(z)
    arrive(1)
    for d in range(1, nb):
        src = (b + d) % nb
        pltpu.make_async_remote_copy(
            src_ref=news.at[s, src], dst_ref=news.at[s, src],
            send_sem=send_n.at[d], recv_sem=recv_n.at[src],
            device_id=(s, src), device_id_type=MESH).wait_recv()
    for d in range(1, ns):
        copy_x(d).start()
    new_all()

    @pl.loop(1, nc - 1)
    def _(i):
        chip = nth_chip(i)
        copy_c(chip, 1 - core, 2, sib).wait_recv()
        pair_all(chip)
        arrive(i + 1)

    def copy_o(j, d):
        return pltpu.make_async_remote_copy(
            src_ref=osend.at[j], dst_ref=orecv.at[s],
            send_sem=send_o.at[d], recv_sem=recv_o.at[s],
            device_id=(j, b), device_id_type=MESH)

    def copy_l(j, d):
        return pltpu.make_async_remote_copy(
            src_ref=lsend.at[j], dst_ref=lrecv.at[s],
            send_sem=send_l.at[d], recv_sem=recv_l.at[s],
            device_id=(j, b), device_id_type=MESH)

    last = nth_chip(nc - 1)
    copy_c(last, 1 - core, 2, sib).wait_recv()
    eye = (lax.broadcasted_iota(jnp.int32, (toks, toks), 0)
           == lax.broadcasted_iota(jnp.int32, (toks, toks), 1))

    @pl.loop(1, ns + 1)
    def _(d):
        j = (s + d) % ns
        for u in range(rows_t // tile):
            pair(last, j * rows_t + u * tile)
        for h in range(hpd):
            rows = pl.ds(pl.multiple_of(j * rows_t + h * toks, toks), toks)
            total = acc_s[rows, HD:]
            osend[j, h * toks:(h + 1) * toks, :] = (acc_s[rows, 0:HD] / total).astype(jnp.bfloat16)
            lse = m_s[rows, :] * scale + jnp.log2(total)
            lsend[j, h:h + 1, :] = jnp.sum(jnp.where(eye, lse, 0.0), axis=0, keepdims=True)

        @pl.when(d < ns)
        def _():
            copy_o(j, d).start()
            copy_l(j, d).start()

    for d in range(1, ns):
        src = (s + d) % ns
        pltpu.make_async_remote_copy(
            src_ref=news.at[src], dst_ref=news.at[src],
            send_sem=send_x.at[d], recv_sem=recv_x.at[src],
            device_id=(src, b), device_id_type=MESH).wait_recv()
    pages = owner_ref.shape[0]
    total_rows = pages * PAGE
    owned = (owner_ref[...] == me).astype(jnp.float32)
    count = jnp.sum(owned, axis=0, keepdims=True)
    owned_b = jnp.broadcast_to(owned, (pages, 128)).astype(jnp.bfloat16)
    up = lax.broadcasted_iota(jnp.int32, (pages, pages), 0)
    across = lax.broadcasted_iota(jnp.int32, (pages, pages), 1)
    over_first = (((0,), (0,)), ((), ()))
    earlier = lax.dot_general(owned_b, jnp.where(up < across, 1.0, 0.0).astype(jnp.bfloat16),
                              over_first, preferred_element_type=jnp.float32)
    here = lax.dot_general(owned_b, jnp.where(up == across, 1.0, 0.0).astype(jnp.bfloat16),
                           over_first, preferred_element_type=jnp.float32)
    place = jnp.where(here > 0.5, earlier, 128.0)[0:16, :].astype(jnp.bfloat16)

    def row_at(shape, axis):
        i = lax.broadcasted_iota(jnp.int32, shape, axis)
        group = i // (nb * part)
        rest = i % (nb * part)
        return (rest // part) * toks + group * part + rest % part

    spread = (row_at((pages, total_rows), 1) // PAGE
              == lax.broadcasted_iota(jnp.int32, (pages, total_rows), 0))
    placed = jnp.dot(place, jnp.where(spread, 1.0, 0.0).astype(jnp.bfloat16),
                     preferred_element_type=jnp.float32)
    filled = len_ref[me].astype(jnp.float32)
    dest = filled + placed[0:1, :] * PAGE + (row_at((1, total_rows), 1) % PAGE).astype(jnp.float32)
    tail = slots - low
    slot = (low + lax.broadcasted_iota(jnp.int32, (tail, 1), 0)).astype(jnp.float32)
    hot = jnp.where(slot == dest, 1.0, 0.0).astype(jnp.bfloat16)
    rows = news[...].reshape(total_rows, 2 * HD)
    picked = jnp.dot(hot, rows, preferred_element_type=jnp.float32)
    is_new = (slot >= filled) & (slot < filled + PAGE * count)
    cout_ref[0:low, :] = cache_ref[0:low, :]
    cout_ref[low:, :] = jnp.where(is_new, picked, cache_ref[low:, :].astype(jnp.float32)).astype(jnp.bfloat16)

    orecv[s, :, :] = osend[s, :, :]
    lrecv[s, :, :] = lsend[s, :, :]
    for d in range(1, ns):
        src = (s + d) % ns
        pltpu.make_async_remote_copy(
            src_ref=osend.at[src], dst_ref=orecv.at[src],
            send_sem=send_o.at[d], recv_sem=recv_o.at[src],
            device_id=(src, b), device_id_type=MESH).wait_recv()
        pltpu.make_async_remote_copy(
            src_ref=lsend.at[src], dst_ref=lrecv.at[src],
            send_sem=send_l.at[d], recv_sem=recv_l.at[src],
            device_id=(src, b), device_id_type=MESH).wait_recv()
    for h in range(hpd):
        lses = [lrecv[g, h:h + 1, :] for g in range(ns)]
        top = functools.reduce(jnp.maximum, lses)
        shares = [jnp.exp2(v - top) for v in lses]
        whole = functools.reduce(jnp.add, shares)
        out = jnp.zeros((toks, HD), jnp.float32)
        for g in range(ns):
            share = jnp.broadcast_to(shares[g] / whole, (toks, toks)).T
            out = out + share[:, 0:1] * orecv[g, h * toks:(h + 1) * toks, :].astype(jnp.float32)
        attn_ref[:, h * HD:(h + 1) * HD] = out.astype(jnp.bfloat16)

    for d in range(1, nb):
        copy_n(d).wait_send()
    for d in range(1, ns):
        copy_x(d).wait_send()
        copy_o((s + d) % ns, d).wait_send()
        copy_l((s + d) % ns, d).wait_send()

    @pl.loop(0, nc)
    def _(k):
        copy_c(k, core, 2, sib).wait_send()

        @pl.when((k <= z) & (z < nc - 1))
        def _():
            copy_c(k, core, 1, b + 2).wait_send()

        @pl.when((k >= z) & (z > 0))
        def _():
            copy_c(k, core, 0, b - 2).wait_send()


def solution(mesh):
    ns, nb = mesh.shape["seg"], mesh.shape["blk"]
    nc = nb // 2

    def on_device(queries, new_kv, cache_kv, cache_len, page_owner):
        toks = queries.shape[0]
        heads = queries.shape[1] // HD
        slots, width = cache_kv.shape
        pages = page_owner.shape[0]
        cap = slots - PAGE * 4 * pages // (ns * nb)
        low = slots // 2
        rows_t = heads // ns * toks
        tile = min(256, rows_t)
        part = toks // ns
        vmem = pl.BlockSpec(memory_space=pltpu.VMEM)
        dma = pltpu.SemaphoreType.DMA
        return pl.pallas_call(
            functools.partial(body, ns, nb, cap, low, tile),
            out_shape=(jax.ShapeDtypeStruct((toks, heads // ns * HD), jnp.bfloat16),
                       jax.ShapeDtypeStruct((slots, width), jnp.bfloat16)),
            in_specs=[pl.BlockSpec(memory_space=pltpu.SMEM), vmem, vmem, vmem, vmem],
            out_specs=(vmem, vmem),
            scratch_shapes=[
                pltpu.VMEM((nc, 2 * cap, width), jnp.bfloat16),
                pltpu.VMEM((ns, nb, part, width), jnp.bfloat16),
                pltpu.VMEM((heads * toks, HD), jnp.bfloat16),
                pltpu.VMEM((heads * toks, 128), jnp.float32),
                pltpu.VMEM((heads * toks, 2 * HD), jnp.float32),
                pltpu.VMEM((ns, rows_t, HD), jnp.bfloat16),
                pltpu.VMEM((ns, 8, toks), jnp.float32),
                pltpu.VMEM((ns, rows_t, HD), jnp.bfloat16),
                pltpu.VMEM((ns, 8, toks), jnp.float32),
                dma((nc, 3)), dma((nc, 2)),
                dma((nb,)), dma((nb,)),
                dma((ns,)), dma((ns,)),
                dma((ns,)), dma((ns,)),
                dma((ns,)), dma((ns,)),
            ],
            compiler_params=pltpu.CompilerParams(
                collective_id=0, has_side_effects=True, vmem_limit_bytes=40 * 1024 * 1024),
            cost_estimate=pl.CostEstimate(
                flops=heads * toks * nb * slots * HD * 4, bytes_accessed=2 * slots * width * 2,
                transcendentals=heads * toks * nb * slots),
        )(cache_len, queries, new_kv, cache_kv, page_owner)

    placed = (P("blk", None), P("blk", None), P(("seg", "blk"), None), P(), P())
    return jax.shard_map(
        on_device,
        mesh=mesh,
        in_specs=placed,
        out_specs=(P("blk", "seg"), P(("seg", "blk"), None)),
        check_vma=False,
    )
```

```python
import functools
import math

import jax
import jax.numpy as jnp
from jax import lax
from jax.experimental import pallas as pl
from jax.experimental.pallas import tpu as pltpu
from jax.sharding import PartitionSpec as P

PAGE = 8
HD = 128
NEG = -1e30
MESH = pl.DeviceIdType.MESH


def body(ns, nb, cap, low, tile, len_ref, q_ref, new_ref, cache_ref, owner_ref, attn_ref, cout_ref,
         held, news, cache_v, q_s, m_s, acc_s, osend, lsend, orecv, lrecv,
         send_c, recv_c, send_n, recv_n, send_x, recv_x, send_o, recv_o, send_l, recv_l, in_sem):
    s = lax.axis_index("seg")
    b = lax.axis_index("blk")
    nc = nb // 2
    z = b // 2
    core = b % 2
    sib = z * 2 + 1 - core
    me = s * nb + b
    toks = q_ref.shape[0]
    heads = q_ref.shape[1] // HD
    part_rows = pl.ds(pl.multiple_of(s * (toks // ns), 16), toks // ns)
    hpd = heads // ns
    rows_t = hpd * toks
    half = heads * toks // 2
    part = toks // ns
    slots = cache_ref.shape[0]
    scale = math.log2(math.e) / math.sqrt(HD)

    def shard(chip, c):
        return held.at[chip, pl.ds(pl.multiple_of(c * cap, 16), cap)]

    barrier = pltpu.get_barrier_semaphore()
    for d in range(1, nb):
        pl.semaphore_signal(barrier, inc=1, device_id=(s, (b + d) % nb), device_id_type=MESH)
    for d in range(1, ns):
        pl.semaphore_signal(barrier, inc=1, device_id=((s + d) % ns, b), device_id_type=MESH)
    own_in = pltpu.make_async_copy(cache_ref.at[pl.ds(0, cap)], shard(z, core), in_sem.at[0])
    new_in = pltpu.make_async_copy(new_ref.at[part_rows], news.at[s, b], in_sem.at[1])
    tail_in = pltpu.make_async_copy(cache_ref, cache_v, in_sem.at[2])
    q_in = [pltpu.make_async_copy(q_ref.at[:, pl.ds(h * HD, HD)], q_s.at[pl.ds(h * toks, toks)], in_sem.at[3 + h])
            for h in range(heads)]
    own_in.start()
    new_in.start()
    for copy in q_in:
        copy.start()
    tail_in.start()
    own_in.wait()
    new_in.wait()
    pl.semaphore_wait(barrier, nb + ns - 2)

    def copy_c(chip, c, way, target):
        return pltpu.make_async_remote_copy(
            src_ref=shard(chip, c), dst_ref=shard(chip, c),
            send_sem=send_c.at[chip, way], recv_sem=recv_c.at[chip, c],
            device_id=(s, target), device_id_type=MESH)

    def copy_n(d):
        return pltpu.make_async_remote_copy(
            src_ref=news.at[s, b], dst_ref=news.at[s, b],
            send_sem=send_n.at[d], recv_sem=recv_n.at[b],
            device_id=(s, (b + d) % nb), device_id_type=MESH)

    def copy_x(d):
        return pltpu.make_async_remote_copy(
            src_ref=news.at[s], dst_ref=news.at[s],
            send_sem=send_x.at[d], recv_sem=recv_x.at[s],
            device_id=((s + d) % ns, b), device_id_type=MESH)

    copy_c(z, core, 2, sib).start()

    @pl.when(z > 0)
    def _():
        copy_c(z, core, 0, b - 2).start()

    @pl.when(z < nc - 1)
    def _():
        copy_c(z, core, 1, b + 2).start()

    for d in range(1, nb):
        copy_n(d).start()

    m_s[...] = jnp.full_like(m_s, NEG)
    acc_s[...] = jnp.zeros_like(acc_s)

    def online(tiles, keys, vals, valid):
        tiles = [pl.ds(pl.multiple_of(row, tile), tile) for row in tiles]
        n = keys.shape[0]
        olds = [m_s[rows, :] for rows in tiles]
        vaug = jnp.concatenate([vals, jnp.ones_like(vals)], axis=1)

        def score(rows):
            return lax.dot_general(q_s[rows, :], keys, (((1,), (1,)), ((), ())),
                                   preferred_element_type=jnp.float32)

        ahead = score(tiles[0])
        for u, rows in enumerate(tiles):
            sc = ahead
            if u + 1 < len(tiles):
                ahead = score(tiles[u + 1])
            parts = []
            for g in range(n // 128):
                piece = sc[:, g * 128:(g + 1) * 128]
                mask = valid(g)
                parts.append(piece if mask is None else jnp.where(mask, piece, NEG))
            top = functools.reduce(jnp.maximum, parts)
            new = jnp.maximum(olds[u], jnp.max(top, axis=1, keepdims=True))
            p = jnp.concatenate(
                [jnp.exp2((piece - new) * scale).astype(jnp.bfloat16) for piece in parts], axis=1)
            fix = jnp.exp2((olds[u] - new) * scale)
            pv = jnp.dot(p, vaug, preferred_element_type=jnp.float32)
            m_s[rows, :] = new
            acc_s[rows, 0:HD] = acc_s[rows, 0:HD] * fix + pv[:, 0:HD]
            acc_s[rows, HD:] = acc_s[rows, HD:] * fix + pv[:, HD:]

    def pair(chip, tiles):
        len0 = len_ref[s * nb + chip * 2]
        len1 = len_ref[s * nb + chip * 2 + 1]

        def valid(g):
            lo, hi = g * 128, g * 128 + 128
            if all(c % cap < low for c in range(lo, hi)):
                return None
            col = lo + lax.broadcasted_iota(jnp.int32, (1, 128), 1)
            return col < jnp.where(col < cap, len0, cap + len1)

        online(tiles, held[chip, :, 0:HD], held[chip, :, HD:], valid)

    def pair_all(chip):
        @pl.loop(0, 2)
        def _(j):
            pair(chip, [j * half + row for row in range(0, half, tile)])

    def new_all():
        def mask_for(g):
            col = g * 128 + lax.broadcasted_iota(jnp.int32, (1, 128), 1)
            pos = (col // part) * toks + s * part + col % part
            tok = b * toks + lax.broadcasted_iota(jnp.int32, (tile, 1), 0) % toks
            return pos <= tok

        @pl.loop(0, 2)
        def _(j):
            rows = news[s].reshape(nb * part, 2 * HD)
            online([j * half + row for row in range(0, half, tile)], rows[:, 0:HD], rows[:, HD:], mask_for)

    def nth_chip(i):
        short = jnp.minimum(z, nc - 1 - z)
        far = i - short
        both = jnp.where(i % 2 == 1, z - (i + 1) // 2, z + (i + 1) // 2)
        single = jnp.where(2 * z < nc, z + far, z - far)
        return jnp.where(i <= 2 * short, both, single)

    def arrive(k):
        @pl.when(z - k >= 0)
        def _():
            copy_c(z - k, core, 1, b).wait_recv()

            @pl.when(z < nc - 1)
            def _():
                copy_c(z - k, core, 1, b + 2).start()
            copy_c(z - k, core, 2, sib).start()

        @pl.when(z + k < nc)
        def _():
            copy_c(z + k, core, 0, b).wait_recv()

            @pl.when(z > 0)
            def _():
                copy_c(z + k, core, 0, b - 2).start()
            copy_c(z + k, core, 2, sib).start()

    for copy in q_in:
        copy.wait()
    copy_c(z, 1 - core, 2, sib).wait_recv()
    pair_all(z)
    arrive(1)
    for d in range(1, nb):
        src = (b + d) % nb
        pltpu.make_async_remote_copy(
            src_ref=news.at[s, src], dst_ref=news.at[s, src],
            send_sem=send_n.at[d], recv_sem=recv_n.at[src],
            device_id=(s, src), device_id_type=MESH).wait_recv()
    for d in range(1, ns):
        copy_x(d).start()
    new_all()

    @pl.loop(1, nc - 1)
    def _(i):
        chip = nth_chip(i)
        copy_c(chip, 1 - core, 2, sib).wait_recv()
        pair_all(chip)
        arrive(i + 1)

    def copy_o(j, d):
        return pltpu.make_async_remote_copy(
            src_ref=osend.at[j], dst_ref=orecv.at[s],
            send_sem=send_o.at[d], recv_sem=recv_o.at[s],
            device_id=(j, b), device_id_type=MESH)

    def copy_l(j, d):
        return pltpu.make_async_remote_copy(
            src_ref=lsend.at[j], dst_ref=lrecv.at[s],
            send_sem=send_l.at[d], recv_sem=recv_l.at[s],
            device_id=(j, b), device_id_type=MESH)

    last = nth_chip(nc - 1)
    copy_c(last, 1 - core, 2, sib).wait_recv()
    eye = (lax.broadcasted_iota(jnp.int32, (toks, toks), 0)
           == lax.broadcasted_iota(jnp.int32, (toks, toks), 1))

    @pl.loop(1, ns + 1)
    def _(d):
        j = (s + d) % ns
        pair(last, [j * rows_t + row for row in range(0, rows_t, tile)])
        for h in range(hpd):
            rows = pl.ds(pl.multiple_of(j * rows_t + h * toks, toks), toks)
            total = acc_s[rows, HD:]
            osend[j, h * toks:(h + 1) * toks, :] = (acc_s[rows, 0:HD] / total).astype(jnp.bfloat16)
            lse = m_s[rows, :] * scale + jnp.log2(total)
            lsend[j, h:h + 1, :] = jnp.sum(jnp.where(eye, lse, 0.0), axis=0, keepdims=True)

        @pl.when(d < ns)
        def _():
            copy_o(j, d).start()
            copy_l(j, d).start()

    for d in range(1, ns):
        src = (s + d) % ns
        pltpu.make_async_remote_copy(
            src_ref=news.at[src], dst_ref=news.at[src],
            send_sem=send_x.at[d], recv_sem=recv_x.at[src],
            device_id=(src, b), device_id_type=MESH).wait_recv()
    pages = owner_ref.shape[1]
    total_rows = pages * PAGE
    owned = jnp.where(owner_ref[...] == me, 1.0, 0.0)
    count = jnp.sum(owned, axis=1, keepdims=True)
    owned_b = jnp.broadcast_to(owned, (16, pages))
    up = lax.broadcasted_iota(jnp.int32, (pages, pages), 0)
    across = lax.broadcasted_iota(jnp.int32, (pages, pages), 1)
    earlier = jnp.dot(owned_b.astype(jnp.bfloat16), jnp.where(up < across, 1.0, 0.0).astype(jnp.bfloat16),
                      preferred_element_type=jnp.float32)
    place = jnp.where(owned_b > 0.5, earlier, 128.0).astype(jnp.bfloat16)

    def row_at(shape, axis):
        i = lax.broadcasted_iota(jnp.int32, shape, axis)
        group = i // (nb * part)
        rest = i % (nb * part)
        return (rest // part) * toks + group * part + rest % part

    spread = (row_at((pages, total_rows), 1) // PAGE
              == lax.broadcasted_iota(jnp.int32, (pages, total_rows), 0))
    placed = jnp.dot(place, jnp.where(spread, 1.0, 0.0).astype(jnp.bfloat16),
                     preferred_element_type=jnp.float32)
    filled = len_ref[me].astype(jnp.float32)
    dest = filled + placed[0:1, :] * PAGE + (row_at((1, total_rows), 1) % PAGE).astype(jnp.float32)
    tail = slots - low
    slot = (low + lax.broadcasted_iota(jnp.int32, (tail, 1), 0)).astype(jnp.float32)
    hot = jnp.where(slot == dest, 1.0, 0.0).astype(jnp.bfloat16)
    rows = news[...].reshape(total_rows, 2 * HD)
    picked = jnp.dot(hot, rows, preferred_element_type=jnp.float32)
    is_new = (slot >= filled) & (slot < filled + PAGE * count)
    tail_in.wait()
    cout_ref[0:low, :] = cache_v[0:low, :]
    cout_ref[low:, :] = jnp.where(is_new, picked, cache_v[low:, :].astype(jnp.float32)).astype(jnp.bfloat16)

    orecv[s, :, :] = osend[s, :, :]
    lrecv[s, :, :] = lsend[s, :, :]
    for d in range(1, ns):
        src = (s + d) % ns
        pltpu.make_async_remote_copy(
            src_ref=osend.at[src], dst_ref=orecv.at[src],
            send_sem=send_o.at[d], recv_sem=recv_o.at[src],
            device_id=(src, b), device_id_type=MESH).wait_recv()
        pltpu.make_async_remote_copy(
            src_ref=lsend.at[src], dst_ref=lrecv.at[src],
            send_sem=send_l.at[d], recv_sem=recv_l.at[src],
            device_id=(src, b), device_id_type=MESH).wait_recv()
    for h in range(hpd):
        lses = [lrecv[g, h:h + 1, :] for g in range(ns)]
        top = functools.reduce(jnp.maximum, lses)
        shares = [jnp.exp2(v - top) for v in lses]
        whole = functools.reduce(jnp.add, shares)
        out = jnp.zeros((toks, HD), jnp.float32)
        for g in range(ns):
            share = jnp.broadcast_to(shares[g] / whole, (HD, toks)).T
            out = out + share * orecv[g, h * toks:(h + 1) * toks, :].astype(jnp.float32)
        attn_ref[:, h * HD:(h + 1) * HD] = out.astype(jnp.bfloat16)

    for d in range(1, nb):
        copy_n(d).wait_send()
    for d in range(1, ns):
        copy_x(d).wait_send()
        copy_o((s + d) % ns, d).wait_send()
        copy_l((s + d) % ns, d).wait_send()

    @pl.loop(0, nc)
    def _(k):
        copy_c(k, core, 2, sib).wait_send()

        @pl.when((k <= z) & (z < nc - 1))
        def _():
            copy_c(k, core, 1, b + 2).wait_send()

        @pl.when((k >= z) & (z > 0))
        def _():
            copy_c(k, core, 0, b - 2).wait_send()


def solution(mesh):
    ns, nb = mesh.shape["seg"], mesh.shape["blk"]
    nc = nb // 2

    def on_device(queries, new_kv, cache_kv, cache_len, page_owner):
        toks = queries.shape[0]
        heads = queries.shape[1] // HD
        slots, width = cache_kv.shape
        pages = page_owner.shape[0]
        cap = slots - PAGE * 4 * pages // (ns * nb)
        low = slots // 2
        rows_t = heads // ns * toks
        tile = min(256, rows_t)
        part = toks // ns
        vmem = pl.BlockSpec(memory_space=pltpu.VMEM)
        hbm = pl.BlockSpec(memory_space=pltpu.HBM)
        dma = pltpu.SemaphoreType.DMA
        return pl.pallas_call(
            functools.partial(body, ns, nb, cap, low, tile),
            out_shape=(jax.ShapeDtypeStruct((toks, heads // ns * HD), jnp.bfloat16),
                       jax.ShapeDtypeStruct((slots, width), jnp.bfloat16)),
            in_specs=[pl.BlockSpec(memory_space=pltpu.SMEM), hbm, hbm, hbm, vmem],
            out_specs=(vmem, vmem),
            scratch_shapes=[
                pltpu.VMEM((nc, 2 * cap, width), jnp.bfloat16),
                pltpu.VMEM((ns, nb, part, width), jnp.bfloat16),
                pltpu.VMEM((slots, width), jnp.bfloat16),
                pltpu.VMEM((heads * toks, HD), jnp.bfloat16),
                pltpu.VMEM((heads * toks, 128), jnp.float32),
                pltpu.VMEM((heads * toks, 2 * HD), jnp.float32),
                pltpu.VMEM((ns, rows_t, HD), jnp.bfloat16),
                pltpu.VMEM((ns, 8, toks), jnp.float32),
                pltpu.VMEM((ns, rows_t, HD), jnp.bfloat16),
                pltpu.VMEM((ns, 8, toks), jnp.float32),
                dma((nc, 3)), dma((nc, 2)),
                dma((nb,)), dma((nb,)),
                dma((ns,)), dma((ns,)),
                dma((ns,)), dma((ns,)),
                dma((ns,)), dma((ns,)), dma((3 + heads,)),
            ],
            compiler_params=pltpu.CompilerParams(
                collective_id=0, has_side_effects=True, vmem_limit_bytes=63 * 1024 * 1024),
            cost_estimate=pl.CostEstimate(
                flops=heads * toks * nb * slots * HD * 4, bytes_accessed=2 * slots * width * 2,
                transcendentals=heads * toks * nb * slots),
        )(cache_len, queries, new_kv, cache_kv, page_owner.reshape(1, pages))

    placed = (P("blk", None), P("blk", None), P(("seg", "blk"), None), P(), P())
    return jax.shard_map(
        on_device,
        mesh=mesh,
        in_specs=placed,
        out_specs=(P("blk", "seg"), P(("seg", "blk"), None)),
        check_vma=False,
    )
```

```python
import functools
import math

import jax
import jax.numpy as jnp
from jax import lax
from jax.experimental import pallas as pl
from jax.experimental.pallas import tpu as pltpu
from jax.sharding import PartitionSpec as P

PAGE = 8
HD = 128
NEG = -1e30
MESH = pl.DeviceIdType.MESH


def body(ns, nb, cap, low, tile, len_ref, q_ref, new_ref, cache_ref, owner_ref, attn_ref, cout_ref,
         held, news, cache_v, keys_t, q_s, m_s, acc_s, osend, lsend, orecv, lrecv,
         send_c, recv_c, send_n, recv_n, send_x, recv_x, send_o, recv_o, send_l, recv_l, in_sem):
    s = lax.axis_index("seg")
    b = lax.axis_index("blk")
    nc = nb // 2
    z = b // 2
    core = b % 2
    sib = z * 2 + 1 - core
    me = s * nb + b
    toks = q_ref.shape[0]
    heads = q_ref.shape[1] // HD
    part_rows = pl.ds(pl.multiple_of(s * (toks // ns), 16), toks // ns)
    hpd = heads // ns
    rows_t = hpd * toks
    half = heads * toks // 2
    part = toks // ns
    slots = cache_ref.shape[0]
    scale = math.log2(math.e) / math.sqrt(HD)

    def shard(chip, c):
        return held.at[chip, pl.ds(pl.multiple_of(c * cap, 16), cap)]

    barrier = pltpu.get_barrier_semaphore()
    for d in range(1, nc):
        pl.semaphore_signal(barrier, inc=1, device_id=(s, (b + 2 * d) % nb), device_id_type=MESH)
    pl.semaphore_signal(barrier, inc=1, device_id=(s, sib), device_id_type=MESH)
    for d in range(1, ns):
        pl.semaphore_signal(barrier, inc=1, device_id=((s + d) % ns, b), device_id_type=MESH)
    own_in = pltpu.make_async_copy(cache_ref.at[pl.ds(0, cap)], shard(z, core), in_sem.at[0])
    new_in = pltpu.make_async_copy(new_ref.at[part_rows], news.at[s, b], in_sem.at[1])
    tail_in = pltpu.make_async_copy(cache_ref, cache_v, in_sem.at[2])
    q_in = [pltpu.make_async_copy(q_ref.at[:, pl.ds(h * HD, HD)], q_s.at[pl.ds(h * toks, toks)], in_sem.at[3 + h])
            for h in range(heads)]
    own_in.start()
    new_in.start()
    for copy in q_in:
        copy.start()
    tail_in.start()
    own_in.wait()
    new_in.wait()
    pl.semaphore_wait(barrier, nc + ns - 1)

    def copy_c(chip, c, way, target):
        return pltpu.make_async_remote_copy(
            src_ref=shard(chip, c), dst_ref=shard(chip, c),
            send_sem=send_c.at[chip, way], recv_sem=recv_c.at[chip, c],
            device_id=(s, target), device_id_type=MESH)

    def copy_n(d):
        return pltpu.make_async_remote_copy(
            src_ref=news.at[s, b], dst_ref=news.at[s, b],
            send_sem=send_n.at[d], recv_sem=recv_n.at[b],
            device_id=(s, (b + 2 * d) % nb), device_id_type=MESH)

    def copy_f(d):
        src = (b + 2 * d) % nb
        return pltpu.make_async_remote_copy(
            src_ref=news.at[s, src], dst_ref=news.at[s, src],
            send_sem=send_n.at[nc + d], recv_sem=recv_n.at[src],
            device_id=(s, sib), device_id_type=MESH)

    def arrived_n(src):
        pltpu.make_async_remote_copy(
            src_ref=news.at[s, src], dst_ref=news.at[s, src],
            send_sem=send_n.at[0], recv_sem=recv_n.at[src],
            device_id=(s, sib), device_id_type=MESH).wait_recv()

    def copy_x(d):
        return pltpu.make_async_remote_copy(
            src_ref=news.at[s], dst_ref=news.at[s],
            send_sem=send_x.at[d], recv_sem=recv_x.at[s],
            device_id=((s + d) % ns, b), device_id_type=MESH)

    @pl.when(z > 0)
    def _():
        copy_c(z, core, 0, b - 2).start()

    @pl.when(z < nc - 1)
    def _():
        copy_c(z, core, 1, b + 2).start()

    copy_c(z, core, 2, sib).start()
    copy_f(0).start()
    for d in range(1, nc):
        copy_n(d).start()

    m_s[...] = jnp.full_like(m_s, NEG)
    acc_s[...] = jnp.zeros_like(acc_s)

    def online(tiles, vals, valid):
        tiles = [pl.ds(pl.multiple_of(row, tile), tile) for row in tiles]
        n = vals.shape[0]
        olds = [m_s[rows, :] for rows in tiles]
        vaug = jnp.concatenate([vals, jnp.ones_like(vals)], axis=1)

        def score(rows):
            return jnp.dot(q_s[rows, :], keys_t[:, 0:n], preferred_element_type=jnp.float32)

        ahead = score(tiles[0])
        for u, rows in enumerate(tiles):
            sc = ahead
            if u + 1 < len(tiles):
                ahead = score(tiles[u + 1])
            parts = []
            for g in range(n // 128):
                piece = sc[:, g * 128:(g + 1) * 128]
                mask = valid(g)
                parts.append(piece if mask is None else jnp.where(mask, piece, NEG))
            top = functools.reduce(jnp.maximum, parts)
            new = jnp.maximum(olds[u], jnp.max(top, axis=1, keepdims=True))
            p = jnp.concatenate(
                [jnp.exp2((piece - new) * scale).astype(jnp.bfloat16) for piece in parts], axis=1)
            fix = jnp.exp2((olds[u] - new) * scale)
            pv = jnp.dot(p, vaug, preferred_element_type=jnp.float32)
            m_s[rows, :] = new
            acc_s[rows, 0:HD] = acc_s[rows, 0:HD] * fix + pv[:, 0:HD]
            acc_s[rows, HD:] = acc_s[rows, HD:] * fix + pv[:, HD:]

    def pair(chip, tiles):
        len0 = len_ref[s * nb + chip * 2]
        len1 = len_ref[s * nb + chip * 2 + 1]

        def valid(g):
            lo, hi = g * 128, g * 128 + 128
            if all(c % cap < low for c in range(lo, hi)):
                return None
            col = lo + lax.broadcasted_iota(jnp.int32, (1, 128), 1)
            return col < jnp.where(col < cap, len0, cap + len1)

        online(tiles, held[chip, :, HD:], valid)

    def pair_all(chip, after=lambda j: None):
        keys_t[:, 0:2 * cap] = held[chip, :, 0:HD].T

        @pl.loop(0, 2)
        def _(j):
            pair(chip, [j * half + row for row in range(0, half, tile)])
            after(j)

    def new_all():
        def mask_for(g):
            col = g * 128 + lax.broadcasted_iota(jnp.int32, (1, 128), 1)
            pos = (col // part) * toks + s * part + col % part
            tok = b * toks + lax.broadcasted_iota(jnp.int32, (tile, 1), 0) % toks
            return pos <= tok

        keys_t[:, 0:nb * part] = news[s].reshape(nb * part, 2 * HD)[:, 0:HD].T

        @pl.loop(0, 2)
        def _(j):
            rows = news[s].reshape(nb * part, 2 * HD)
            online([j * half + row for row in range(0, half, tile)], rows[:, HD:], mask_for)

    def nth_chip(i):
        short = jnp.minimum(z, nc - 1 - z)
        far = i - short
        both = jnp.where(i % 2 == 1, z - (i + 1) // 2, z + (i + 1) // 2)
        single = jnp.where(2 * z < nc, z + far, z - far)
        return jnp.where(i <= 2 * short, both, single)

    def arrive(k):
        @pl.when(z - k >= 0)
        def _():
            copy_c(z - k, core, 1, b).wait_recv()

            @pl.when(z < nc - 1)
            def _():
                copy_c(z - k, core, 1, b + 2).start()
            copy_c(z - k, core, 2, sib).start()

        @pl.when(z + k < nc)
        def _():
            copy_c(z + k, core, 0, b).wait_recv()

            @pl.when(z > 0)
            def _():
                copy_c(z + k, core, 0, b - 2).start()
            copy_c(z + k, core, 2, sib).start()

    for copy in q_in:
        copy.wait()
    copy_c(z, 1 - core, 2, sib).wait_recv()
    pair_all(z)
    arrive(1)
    for d in range(1, nc):
        arrived_n((b + 2 * d) % nb)
        copy_f(d).start()
    for d in range(nc):
        arrived_n((sib + 2 * d) % nb)
    for d in range(1, ns):
        copy_x(d).start()
    new_all()

    @pl.loop(1, nc - 1)
    def _(i):
        chip = nth_chip(i)
        copy_c(chip, 1 - core, 2, sib).wait_recv()

        def after(j):
            @pl.when(j == jnp.where((z > 0) & (z < nc - 1), 0, 1))
            def _():
                arrive(i + 1)
        pair_all(chip, after)

    def copy_o(j, d):
        return pltpu.make_async_remote_copy(
            src_ref=osend.at[j], dst_ref=orecv.at[s],
            send_sem=send_o.at[d], recv_sem=recv_o.at[s],
            device_id=(j, b), device_id_type=MESH)

    def copy_l(j, d):
        return pltpu.make_async_remote_copy(
            src_ref=lsend.at[j], dst_ref=lrecv.at[s],
            send_sem=send_l.at[d], recv_sem=recv_l.at[s],
            device_id=(j, b), device_id_type=MESH)

    last = nth_chip(nc - 1)
    copy_c(last, 1 - core, 2, sib).wait_recv()
    keys_t[:, 0:2 * cap] = held[last, :, 0:HD].T
    eye = (lax.broadcasted_iota(jnp.int32, (toks, toks), 0)
           == lax.broadcasted_iota(jnp.int32, (toks, toks), 1))

    @pl.loop(1, ns + 1)
    def _(d):
        j = (s + d) % ns
        pair(last, [j * rows_t + row for row in range(0, rows_t, tile)])
        for h in range(hpd):
            rows = pl.ds(pl.multiple_of(j * rows_t + h * toks, toks), toks)
            total = acc_s[rows, HD:]
            osend[j, h * toks:(h + 1) * toks, :] = (acc_s[rows, 0:HD] / total).astype(jnp.bfloat16)
            lse = m_s[rows, :] * scale + jnp.log2(total)
            lsend[j, h:h + 1, :] = jnp.sum(jnp.where(eye, lse, 0.0), axis=0, keepdims=True)

        @pl.when(d < ns)
        def _():
            copy_o(j, d).start()
            copy_l(j, d).start()

    for d in range(1, ns):
        src = (s + d) % ns
        pltpu.make_async_remote_copy(
            src_ref=news.at[src], dst_ref=news.at[src],
            send_sem=send_x.at[d], recv_sem=recv_x.at[src],
            device_id=(src, b), device_id_type=MESH).wait_recv()
    pages = owner_ref.shape[1]
    total_rows = pages * PAGE
    owned = jnp.where(owner_ref[...] == me, 1.0, 0.0)
    count = jnp.sum(owned, axis=1, keepdims=True)
    owned_b = jnp.broadcast_to(owned, (16, pages))
    up = lax.broadcasted_iota(jnp.int32, (pages, pages), 0)
    across = lax.broadcasted_iota(jnp.int32, (pages, pages), 1)
    earlier = jnp.dot(owned_b.astype(jnp.bfloat16), jnp.where(up < across, 1.0, 0.0).astype(jnp.bfloat16),
                      preferred_element_type=jnp.float32)
    place = jnp.where(owned_b > 0.5, earlier, 128.0).astype(jnp.bfloat16)

    def row_at(shape, axis):
        i = lax.broadcasted_iota(jnp.int32, shape, axis)
        group = i // (nb * part)
        rest = i % (nb * part)
        return (rest // part) * toks + group * part + rest % part

    spread = (row_at((pages, total_rows), 1) // PAGE
              == lax.broadcasted_iota(jnp.int32, (pages, total_rows), 0))
    placed = jnp.dot(place, jnp.where(spread, 1.0, 0.0).astype(jnp.bfloat16),
                     preferred_element_type=jnp.float32)
    filled = len_ref[me].astype(jnp.float32)
    dest = filled + placed[0:1, :] * PAGE + (row_at((1, total_rows), 1) % PAGE).astype(jnp.float32)
    tail = slots - low
    slot = (low + lax.broadcasted_iota(jnp.int32, (tail, 1), 0)).astype(jnp.float32)
    hot = jnp.where(slot == dest, 1.0, 0.0).astype(jnp.bfloat16)
    rows = news[...].reshape(total_rows, 2 * HD)
    picked = jnp.dot(hot, rows, preferred_element_type=jnp.float32)
    is_new = (slot >= filled) & (slot < filled + PAGE * count)
    tail_in.wait()
    cout_ref[0:low, :] = cache_v[0:low, :]
    cout_ref[low:, :] = jnp.where(is_new, picked, cache_v[low:, :].astype(jnp.float32)).astype(jnp.bfloat16)

    orecv[s, :, :] = osend[s, :, :]
    lrecv[s, :, :] = lsend[s, :, :]
    for d in range(1, ns):
        src = (s + d) % ns
        pltpu.make_async_remote_copy(
            src_ref=osend.at[src], dst_ref=orecv.at[src],
            send_sem=send_o.at[d], recv_sem=recv_o.at[src],
            device_id=(src, b), device_id_type=MESH).wait_recv()
        pltpu.make_async_remote_copy(
            src_ref=lsend.at[src], dst_ref=lrecv.at[src],
            send_sem=send_l.at[d], recv_sem=recv_l.at[src],
            device_id=(src, b), device_id_type=MESH).wait_recv()
    for h in range(hpd):
        lses = [lrecv[g, h:h + 1, :] for g in range(ns)]
        top = functools.reduce(jnp.maximum, lses)
        shares = [jnp.exp2(v - top) for v in lses]
        whole = functools.reduce(jnp.add, shares)
        out = jnp.zeros((toks, HD), jnp.float32)
        for g in range(ns):
            share = jnp.broadcast_to(shares[g] / whole, (HD, toks)).T
            out = out + share * orecv[g, h * toks:(h + 1) * toks, :].astype(jnp.float32)
        attn_ref[:, h * HD:(h + 1) * HD] = out.astype(jnp.bfloat16)

    copy_f(0).wait_send()
    for d in range(1, nc):
        copy_n(d).wait_send()
        copy_f(d).wait_send()
    for d in range(1, ns):
        copy_x(d).wait_send()
        copy_o((s + d) % ns, d).wait_send()
        copy_l((s + d) % ns, d).wait_send()

    @pl.loop(0, nc)
    def _(k):
        copy_c(k, core, 2, sib).wait_send()

        @pl.when((k <= z) & (z < nc - 1))
        def _():
            copy_c(k, core, 1, b + 2).wait_send()

        @pl.when((k >= z) & (z > 0))
        def _():
            copy_c(k, core, 0, b - 2).wait_send()


def solution(mesh):
    ns, nb = mesh.shape["seg"], mesh.shape["blk"]
    nc = nb // 2

    def on_device(queries, new_kv, cache_kv, cache_len, page_owner):
        toks = queries.shape[0]
        heads = queries.shape[1] // HD
        slots, width = cache_kv.shape
        pages = page_owner.shape[0]
        cap = slots - PAGE * 4 * pages // (ns * nb)
        low = slots // 2
        rows_t = heads // ns * toks
        tile = min(256, rows_t)
        part = toks // ns
        vmem = pl.BlockSpec(memory_space=pltpu.VMEM)
        hbm = pl.BlockSpec(memory_space=pltpu.HBM)
        dma = pltpu.SemaphoreType.DMA
        return pl.pallas_call(
            functools.partial(body, ns, nb, cap, low, tile),
            out_shape=(jax.ShapeDtypeStruct((toks, heads // ns * HD), jnp.bfloat16),
                       jax.ShapeDtypeStruct((slots, width), jnp.bfloat16)),
            in_specs=[pl.BlockSpec(memory_space=pltpu.SMEM), hbm, hbm, hbm, vmem],
            out_specs=(vmem, vmem),
            scratch_shapes=[
                pltpu.VMEM((nc, 2 * cap, width), jnp.bfloat16),
                pltpu.VMEM((ns, nb, part, width), jnp.bfloat16),
                pltpu.VMEM((slots, width), jnp.bfloat16),
                pltpu.VMEM((HD, max(2 * cap, nb * part)), jnp.bfloat16),
                pltpu.VMEM((heads * toks, HD), jnp.bfloat16),
                pltpu.VMEM((heads * toks, 128), jnp.float32),
                pltpu.VMEM((heads * toks, 2 * HD), jnp.float32),
                pltpu.VMEM((ns, rows_t, HD), jnp.bfloat16),
                pltpu.VMEM((ns, 8, toks), jnp.float32),
                pltpu.VMEM((ns, rows_t, HD), jnp.bfloat16),
                pltpu.VMEM((ns, 8, toks), jnp.float32),
                dma((nc, 3)), dma((nc, 2)),
                dma((nb,)), dma((nb,)),
                dma((ns,)), dma((ns,)),
                dma((ns,)), dma((ns,)),
                dma((ns,)), dma((ns,)), dma((3 + heads,)),
            ],
            compiler_params=pltpu.CompilerParams(
                collective_id=0, has_side_effects=True, vmem_limit_bytes=63 * 1024 * 1024),
            cost_estimate=pl.CostEstimate(
                flops=heads * toks * nb * slots * HD * 4, bytes_accessed=2 * slots * width * 2,
                transcendentals=heads * toks * nb * slots),
        )(cache_len, queries, new_kv, cache_kv, page_owner.reshape(1, pages))

    placed = (P("blk", None), P("blk", None), P(("seg", "blk"), None), P(), P())
    return jax.shard_map(
        on_device,
        mesh=mesh,
        in_specs=placed,
        out_specs=(P("blk", "seg"), P(("seg", "blk"), None)),
        check_vma=False,
    )
```

```python
import functools
import math

import jax
import jax.numpy as jnp
from jax import lax
from jax.experimental import pallas as pl
from jax.experimental.pallas import tpu as pltpu
from jax.sharding import PartitionSpec as P

PAGE = 8
HD = 128
NEG = -1e30
MESH = pl.DeviceIdType.MESH


def body(ns, nb, cap, low, tile, len_ref, q_ref, new_ref, cache_ref, owner_ref, attn_ref, cout_ref,
         held, news, cache_v, keys_t, q_s, m_s, acc_s, osend, lsend, orecv, lrecv,
         send_c, recv_c, send_n, recv_n, send_x, recv_x, send_o, recv_o, send_l, recv_l, in_sem):
    s = lax.axis_index("seg")
    b = lax.axis_index("blk")
    nc = nb // 2
    z = b // 2
    core = b % 2
    sib = z * 2 + 1 - core
    me = s * nb + b
    toks = q_ref.shape[0]
    heads = q_ref.shape[1] // HD
    part_rows = pl.ds(pl.multiple_of(s * (toks // ns), 16), toks // ns)
    hpd = heads // ns
    rows_t = hpd * toks
    half = heads * toks // 2
    part = toks // ns
    slots = cache_ref.shape[0]
    scale = math.log2(math.e) / math.sqrt(HD)

    def shard(chip, c):
        return held.at[chip, pl.ds(pl.multiple_of(c * cap, 16), cap)]

    barrier = pltpu.get_barrier_semaphore()
    for d in range(1, nc):
        pl.semaphore_signal(barrier, inc=1, device_id=(s, (b + 2 * d) % nb), device_id_type=MESH)
    pl.semaphore_signal(barrier, inc=1, device_id=(s, sib), device_id_type=MESH)
    for d in range(1, ns):
        pl.semaphore_signal(barrier, inc=1, device_id=((s + d) % ns, b), device_id_type=MESH)
    own_in = pltpu.make_async_copy(cache_ref.at[pl.ds(0, cap)], shard(z, core), in_sem.at[0])
    new_in = pltpu.make_async_copy(new_ref.at[part_rows], news.at[s, b], in_sem.at[1])
    tail_in = pltpu.make_async_copy(cache_ref, cache_v, in_sem.at[2])
    q_in = [pltpu.make_async_copy(q_ref.at[:, pl.ds(h * HD, HD)], q_s.at[pl.ds(h * toks, toks)], in_sem.at[3 + h])
            for h in range(heads)]
    own_in.start()
    new_in.start()
    for copy in q_in:
        copy.start()
    tail_in.start()
    own_in.wait()
    new_in.wait()
    pl.semaphore_wait(barrier, nc + ns - 1)

    def copy_c(chip, c, way, target):
        return pltpu.make_async_remote_copy(
            src_ref=shard(chip, c), dst_ref=shard(chip, c),
            send_sem=send_c.at[chip, way], recv_sem=recv_c.at[chip, c],
            device_id=(s, target), device_id_type=MESH)

    def copy_n(d):
        return pltpu.make_async_remote_copy(
            src_ref=news.at[s, b], dst_ref=news.at[s, b],
            send_sem=send_n.at[d], recv_sem=recv_n.at[b],
            device_id=(s, (b + 2 * d) % nb), device_id_type=MESH)

    def copy_f(d):
        src = (b + 2 * d) % nb
        return pltpu.make_async_remote_copy(
            src_ref=news.at[s, src], dst_ref=news.at[s, src],
            send_sem=send_n.at[nc + d], recv_sem=recv_n.at[src],
            device_id=(s, sib), device_id_type=MESH)

    def arrived_n(src):
        pltpu.make_async_remote_copy(
            src_ref=news.at[s, src], dst_ref=news.at[s, src],
            send_sem=send_n.at[0], recv_sem=recv_n.at[src],
            device_id=(s, sib), device_id_type=MESH).wait_recv()

    def copy_x(d):
        return pltpu.make_async_remote_copy(
            src_ref=news.at[s], dst_ref=news.at[s],
            send_sem=send_x.at[d], recv_sem=recv_x.at[s],
            device_id=((s + d) % ns, b), device_id_type=MESH)

    @pl.when(z > 0)
    def _():
        copy_c(z, core, 0, b - 2).start()

    @pl.when(z < nc - 1)
    def _():
        copy_c(z, core, 1, b + 2).start()

    copy_c(z, core, 2, sib).start()
    copy_f(0).start()
    for d in range(1, nc):
        copy_n(d).start()

    m_s[...] = jnp.full_like(m_s, NEG)
    acc_s[...] = jnp.zeros_like(acc_s)

    def online(tiles, vals, valid):
        tiles = [pl.ds(pl.multiple_of(row, tile), tile) for row in tiles]
        n = vals.shape[0]
        olds = [m_s[rows, :] for rows in tiles]
        vaug = jnp.concatenate([vals, jnp.ones_like(vals)], axis=1)

        def score(rows):
            return jnp.dot(q_s[rows, :], keys_t[:, 0:n], preferred_element_type=jnp.float32)

        ahead = score(tiles[0])
        for u, rows in enumerate(tiles):
            sc = ahead
            if u + 1 < len(tiles):
                ahead = score(tiles[u + 1])
            parts = []
            for g in range(n // 128):
                piece = sc[:, g * 128:(g + 1) * 128]
                mask = valid(g)
                parts.append(piece if mask is None else jnp.where(mask, piece, NEG))
            top = functools.reduce(jnp.maximum, parts)
            new = jnp.maximum(olds[u], jnp.max(top, axis=1, keepdims=True))
            p = jnp.concatenate(
                [jnp.exp2((piece - new) * scale).astype(jnp.bfloat16) for piece in parts], axis=1)
            fix = jnp.exp2((olds[u] - new) * scale)
            pv = jnp.dot(p, vaug, preferred_element_type=jnp.float32)
            m_s[rows, :] = new
            acc_s[rows, 0:HD] = acc_s[rows, 0:HD] * fix + pv[:, 0:HD]
            acc_s[rows, HD:] = acc_s[rows, HD:] * fix + pv[:, HD:]

    def pair(chip, tiles):
        len0 = len_ref[s * nb + chip * 2]
        len1 = len_ref[s * nb + chip * 2 + 1]

        def valid(g):
            lo, hi = g * 128, g * 128 + 128
            if all(c % cap < low for c in range(lo, hi)):
                return None
            col = lo + lax.broadcasted_iota(jnp.int32, (1, 128), 1)
            return col < jnp.where(col < cap, len0, cap + len1)

        online(tiles, held[chip, :, HD:], valid)

    def pair_all(chip, after=lambda j: None):
        keys_t[:, 0:2 * cap] = held[chip, :, 0:HD].T

        @pl.loop(0, 2)
        def _(j):
            pair(chip, [j * half + row for row in range(0, half, tile)])
            after(j)

    def new_all():
        def mask_for(g):
            col = g * 128 + lax.broadcasted_iota(jnp.int32, (1, 128), 1)
            pos = (col // part) * toks + s * part + col % part
            tok = b * toks + lax.broadcasted_iota(jnp.int32, (tile, 1), 0) % toks
            return pos <= tok

        keys_t[:, 0:nb * part] = news[s].reshape(nb * part, 2 * HD)[:, 0:HD].T

        @pl.loop(0, 2)
        def _(j):
            rows = news[s].reshape(nb * part, 2 * HD)
            online([j * half + row for row in range(0, half, tile)], rows[:, HD:], mask_for)

    def nth_chip(i):
        short = jnp.minimum(z, nc - 1 - z)
        far = i - short
        both = jnp.where(i % 2 == 1, z - (i + 1) // 2, z + (i + 1) // 2)
        single = jnp.where(2 * z < nc, z + far, z - far)
        return jnp.where(i <= 2 * short, both, single)

    def arrive(k):
        @pl.when(z - k >= 0)
        def _():
            copy_c(z - k, core, 1, b).wait_recv()

            @pl.when(z < nc - 1)
            def _():
                copy_c(z - k, core, 1, b + 2).start()
            copy_c(z - k, core, 2, sib).start()

        @pl.when(z + k < nc)
        def _():
            copy_c(z + k, core, 0, b).wait_recv()

            @pl.when(z > 0)
            def _():
                copy_c(z + k, core, 0, b - 2).start()
            copy_c(z + k, core, 2, sib).start()

    for copy in q_in:
        copy.wait()
    copy_c(z, 1 - core, 2, sib).wait_recv()
    pair_all(z)
    arrive(1)
    for d in range(1, nc):
        arrived_n((b + 2 * d) % nb)
        copy_f(d).start()
    for d in range(nc):
        arrived_n((sib + 2 * d) % nb)
    for d in range(1, ns):
        copy_x(d).start()
    new_all()

    @pl.loop(1, nc - 1)
    def _(i):
        chip = nth_chip(i)
        copy_c(chip, 1 - core, 2, sib).wait_recv()

        def after(j):
            @pl.when(j == jnp.where((z > 0) & (z < nc - 1), 0, 1))
            def _():
                arrive(i + 1)
        pair_all(chip, after)

    def copy_o(j, d):
        return pltpu.make_async_remote_copy(
            src_ref=osend.at[j], dst_ref=orecv.at[s],
            send_sem=send_o.at[d], recv_sem=recv_o.at[s],
            device_id=(j, b), device_id_type=MESH)

    def copy_l(j, d):
        return pltpu.make_async_remote_copy(
            src_ref=lsend.at[j], dst_ref=lrecv.at[s],
            send_sem=send_l.at[d], recv_sem=recv_l.at[s],
            device_id=(j, b), device_id_type=MESH)

    last = nth_chip(nc - 1)
    copy_c(last, 1 - core, 2, sib).wait_recv()
    keys_t[:, 0:2 * cap] = held[last, :, 0:HD].T
    eye = (lax.broadcasted_iota(jnp.int32, (toks, toks), 0)
           == lax.broadcasted_iota(jnp.int32, (toks, toks), 1))

    @pl.loop(1, ns + 1)
    def _(d):
        j = (s + d) % ns
        pair(last, [j * rows_t + row for row in range(0, rows_t, tile)])
        for h in range(hpd):
            rows = pl.ds(pl.multiple_of(j * rows_t + h * toks, toks), toks)
            total = acc_s[rows, HD:]
            osend[j, h * toks:(h + 1) * toks, :] = (acc_s[rows, 0:HD] / total).astype(jnp.bfloat16)
            lse = m_s[rows, :] * scale + jnp.log2(total)
            lsend[j, h:h + 1, :] = jnp.sum(jnp.where(eye, lse, 0.0), axis=0, keepdims=True)

        @pl.when(d < ns)
        def _():
            copy_o(j, d).start()
            copy_l(j, d).start()

    for d in range(1, ns):
        src = (s + d) % ns
        pltpu.make_async_remote_copy(
            src_ref=news.at[src], dst_ref=news.at[src],
            send_sem=send_x.at[d], recv_sem=recv_x.at[src],
            device_id=(src, b), device_id_type=MESH).wait_recv()
    pages = owner_ref.shape[1]
    total_rows = pages * PAGE
    owned = jnp.where(owner_ref[...] == me, 1.0, 0.0)
    count = jnp.sum(owned, axis=1, keepdims=True)
    owned_b = jnp.broadcast_to(owned, (16, pages))
    up = lax.broadcasted_iota(jnp.int32, (pages, pages), 0)
    across = lax.broadcasted_iota(jnp.int32, (pages, pages), 1)
    earlier = jnp.dot(owned_b.astype(jnp.bfloat16), jnp.where(up < across, 1.0, 0.0).astype(jnp.bfloat16),
                      preferred_element_type=jnp.float32)
    place = jnp.where(owned_b > 0.5, earlier, 128.0).astype(jnp.bfloat16)

    def row_at(shape, axis):
        i = lax.broadcasted_iota(jnp.int32, shape, axis)
        group = i // (nb * part)
        rest = i % (nb * part)
        return (rest // part) * toks + group * part + rest % part

    spread = (row_at((pages, total_rows), 1) // PAGE
              == lax.broadcasted_iota(jnp.int32, (pages, total_rows), 0))
    placed = jnp.dot(place, jnp.where(spread, 1.0, 0.0).astype(jnp.bfloat16),
                     preferred_element_type=jnp.float32)
    filled = len_ref[me].astype(jnp.float32)
    dest = filled + placed[0:1, :] * PAGE + (row_at((1, total_rows), 1) % PAGE).astype(jnp.float32)
    tail = slots - low
    slot = (low + lax.broadcasted_iota(jnp.int32, (tail, 1), 0)).astype(jnp.float32)
    hot = jnp.where(slot == dest, 1.0, 0.0).astype(jnp.bfloat16)
    rows = news[...].reshape(total_rows, 2 * HD)
    picked = jnp.dot(hot, rows, preferred_element_type=jnp.float32)
    is_new = (slot >= filled) & (slot < filled + PAGE * count)
    tail_in.wait()
    cout_ref[0:low, :] = cache_v[0:low, :]
    cout_ref[low:, :] = jnp.where(is_new, picked, cache_v[low:, :].astype(jnp.float32)).astype(jnp.bfloat16)

    orecv[s, :, :] = osend[s, :, :]
    lrecv[s, :, :] = lsend[s, :, :]
    for d in range(1, ns):
        src = (s + d) % ns
        pltpu.make_async_remote_copy(
            src_ref=osend.at[src], dst_ref=orecv.at[src],
            send_sem=send_o.at[d], recv_sem=recv_o.at[src],
            device_id=(src, b), device_id_type=MESH).wait_recv()
        pltpu.make_async_remote_copy(
            src_ref=lsend.at[src], dst_ref=lrecv.at[src],
            send_sem=send_l.at[d], recv_sem=recv_l.at[src],
            device_id=(src, b), device_id_type=MESH).wait_recv()
    for h in range(hpd):
        lses = [lrecv[g, h:h + 1, :] for g in range(ns)]
        top = functools.reduce(jnp.maximum, lses)
        shares = [jnp.exp2(v - top) for v in lses]
        whole = functools.reduce(jnp.add, shares)
        out = jnp.zeros((toks, HD), jnp.float32)
        for g in range(ns):
            share = jnp.broadcast_to(shares[g] / whole, (HD, toks)).T
            out = out + share * orecv[g, h * toks:(h + 1) * toks, :].astype(jnp.float32)
        attn_ref[:, h * HD:(h + 1) * HD] = out.astype(jnp.bfloat16)

    copy_f(0).wait_send()
    for d in range(1, nc):
        copy_n(d).wait_send()
        copy_f(d).wait_send()
    for d in range(1, ns):
        copy_x(d).wait_send()
        copy_o((s + d) % ns, d).wait_send()
        copy_l((s + d) % ns, d).wait_send()

    @pl.loop(0, nc)
    def _(k):
        copy_c(k, core, 2, sib).wait_send()

        @pl.when((k <= z) & (z < nc - 1))
        def _():
            copy_c(k, core, 1, b + 2).wait_send()

        @pl.when((k >= z) & (z > 0))
        def _():
            copy_c(k, core, 0, b - 2).wait_send()


def solution(mesh):
    ns, nb = mesh.shape["seg"], mesh.shape["blk"]
    nc = nb // 2

    def on_device(queries, new_kv, cache_kv, cache_len, page_owner):
        toks = queries.shape[0]
        heads = queries.shape[1] // HD
        slots, width = cache_kv.shape
        pages = page_owner.shape[0]
        cap = slots - PAGE * 4 * pages // (ns * nb)
        low = slots // 2
        rows_t = heads // ns * toks
        tile = min(128, rows_t)
        part = toks // ns
        vmem = pl.BlockSpec(memory_space=pltpu.VMEM)
        hbm = pl.BlockSpec(memory_space=pltpu.HBM)
        dma = pltpu.SemaphoreType.DMA
        return pl.pallas_call(
            functools.partial(body, ns, nb, cap, low, tile),
            out_shape=(jax.ShapeDtypeStruct((toks, heads // ns * HD), jnp.bfloat16),
                       jax.ShapeDtypeStruct((slots, width), jnp.bfloat16)),
            in_specs=[pl.BlockSpec(memory_space=pltpu.SMEM), hbm, hbm, hbm, vmem],
            out_specs=(vmem, vmem),
            scratch_shapes=[
                pltpu.VMEM((nc, 2 * cap, width), jnp.bfloat16),
                pltpu.VMEM((ns, nb, part, width), jnp.bfloat16),
                pltpu.VMEM((slots, width), jnp.bfloat16),
                pltpu.VMEM((HD, max(2 * cap, nb * part)), jnp.bfloat16),
                pltpu.VMEM((heads * toks, HD), jnp.bfloat16),
                pltpu.VMEM((heads * toks, 128), jnp.float32),
                pltpu.VMEM((heads * toks, 2 * HD), jnp.float32),
                pltpu.VMEM((ns, rows_t, HD), jnp.bfloat16),
                pltpu.VMEM((ns, 8, toks), jnp.float32),
                pltpu.VMEM((ns, rows_t, HD), jnp.bfloat16),
                pltpu.VMEM((ns, 8, toks), jnp.float32),
                dma((nc, 3)), dma((nc, 2)),
                dma((nb,)), dma((nb,)),
                dma((ns,)), dma((ns,)),
                dma((ns,)), dma((ns,)),
                dma((ns,)), dma((ns,)), dma((3 + heads,)),
            ],
            compiler_params=pltpu.CompilerParams(
                collective_id=0, has_side_effects=True, vmem_limit_bytes=63 * 1024 * 1024),
            cost_estimate=pl.CostEstimate(
                flops=heads * toks * nb * slots * HD * 4, bytes_accessed=2 * slots * width * 2,
                transcendentals=heads * toks * nb * slots),
        )(cache_len, queries, new_kv, cache_kv, page_owner.reshape(1, pages))

    placed = (P("blk", None), P("blk", None), P(("seg", "blk"), None), P(), P())
    return jax.shard_map(
        on_device,
        mesh=mesh,
        in_specs=placed,
        out_specs=(P("blk", "seg"), P(("seg", "blk"), None)),
        check_vma=False,
    )
```

```python
import functools
import math

import jax
import jax.numpy as jnp
from jax import lax
from jax.experimental import pallas as pl
from jax.experimental.pallas import tpu as pltpu
from jax.sharding import PartitionSpec as P

PAGE = 8
HD = 128
NEG = -1e30
MESH = pl.DeviceIdType.MESH


def body(ns, nb, cap, low, tile, len_ref, q_ref, new_ref, cache_ref, owner_ref, attn_ref, cout_ref,
         held, news, cache_v, keys_t, q_s, m_s, acc_s, osend, lsend, orecv, lrecv,
         send_c, recv_c, send_n, recv_n, send_x, recv_x, send_o, recv_o, send_l, recv_l, in_sem):
    s = lax.axis_index("seg")
    b = lax.axis_index("blk")
    nc = nb // 2
    z = b // 2
    core = b % 2
    sib = z * 2 + 1 - core
    me = s * nb + b
    toks = q_ref.shape[0]
    heads = q_ref.shape[1] // HD
    part_rows = pl.ds(pl.multiple_of(s * (toks // ns), 16), toks // ns)
    hpd = heads // ns
    rows_t = hpd * toks
    half = heads * toks // 2
    part = toks // ns
    slots = cache_ref.shape[0]
    scale = math.log2(math.e) / math.sqrt(HD)

    def shard(chip, c):
        return held.at[chip, pl.ds(pl.multiple_of(c * cap, 16), cap)]

    barrier = pltpu.get_barrier_semaphore()
    for d in range(1, nc):
        pl.semaphore_signal(barrier, inc=1, device_id=(s, (b + 2 * d) % nb), device_id_type=MESH)
    pl.semaphore_signal(barrier, inc=1, device_id=(s, sib), device_id_type=MESH)
    for d in range(1, ns):
        pl.semaphore_signal(barrier, inc=1, device_id=((s + d) % ns, b), device_id_type=MESH)
    own_in = pltpu.make_async_copy(cache_ref.at[pl.ds(0, cap)], shard(z, core), in_sem.at[0])
    new_in = pltpu.make_async_copy(new_ref.at[part_rows], news.at[s, b], in_sem.at[1])
    tail_in = pltpu.make_async_copy(cache_ref, cache_v, in_sem.at[2])
    q_in = [pltpu.make_async_copy(q_ref.at[:, pl.ds(h * HD, HD)], q_s.at[pl.ds(h * toks, toks)], in_sem.at[3 + h])
            for h in range(heads)]
    own_in.start()
    new_in.start()
    for copy in q_in:
        copy.start()
    tail_in.start()
    own_in.wait()
    new_in.wait()
    pl.semaphore_wait(barrier, nc + ns - 1)

    def copy_c(chip, c, way, target):
        return pltpu.make_async_remote_copy(
            src_ref=shard(chip, c), dst_ref=shard(chip, c),
            send_sem=send_c.at[chip, way], recv_sem=recv_c.at[chip, c],
            device_id=(s, target), device_id_type=MESH)

    def copy_n(d):
        return pltpu.make_async_remote_copy(
            src_ref=news.at[s, b], dst_ref=news.at[s, b],
            send_sem=send_n.at[d], recv_sem=recv_n.at[b],
            device_id=(s, (b + 2 * d) % nb), device_id_type=MESH)

    def copy_f(d):
        src = (b + 2 * d) % nb
        return pltpu.make_async_remote_copy(
            src_ref=news.at[s, src], dst_ref=news.at[s, src],
            send_sem=send_n.at[nc + d], recv_sem=recv_n.at[src],
            device_id=(s, sib), device_id_type=MESH)

    def arrived_n(src):
        pltpu.make_async_remote_copy(
            src_ref=news.at[s, src], dst_ref=news.at[s, src],
            send_sem=send_n.at[0], recv_sem=recv_n.at[src],
            device_id=(s, sib), device_id_type=MESH).wait_recv()

    def copy_x(d):
        return pltpu.make_async_remote_copy(
            src_ref=news.at[s], dst_ref=news.at[s],
            send_sem=send_x.at[d], recv_sem=recv_x.at[s],
            device_id=((s + d) % ns, b), device_id_type=MESH)

    @pl.when(z > 0)
    def _():
        copy_c(z, core, 0, b - 2).start()

    @pl.when(z < nc - 1)
    def _():
        copy_c(z, core, 1, b + 2).start()

    copy_c(z, core, 2, sib).start()
    copy_f(0).start()
    for d in range(1, nc):
        copy_n(d).start()

    m_s[...] = jnp.full_like(m_s, NEG)
    acc_s[...] = jnp.zeros_like(acc_s)

    def online(tiles, vals, valid):
        tiles = [pl.ds(pl.multiple_of(row, tile), tile) for row in tiles]
        n = vals.shape[0]
        olds = [m_s[rows, :] for rows in tiles]
        vaug = jnp.concatenate([vals, jnp.ones_like(vals)], axis=1)

        def score(rows):
            return jnp.dot(q_s[rows, :], keys_t[:, 0:n], preferred_element_type=jnp.float32)

        ahead = score(tiles[0])
        for u, rows in enumerate(tiles):
            sc = ahead
            if u + 1 < len(tiles):
                ahead = score(tiles[u + 1])
            parts = []
            for g in range(n // 128):
                piece = sc[:, g * 128:(g + 1) * 128]
                mask = valid(g)
                parts.append(piece if mask is None else jnp.where(mask, piece, NEG))
            top = functools.reduce(jnp.maximum, parts)
            new = jnp.maximum(olds[u], jnp.max(top, axis=1, keepdims=True))
            p = jnp.concatenate(
                [jnp.exp2((piece - new) * scale).astype(jnp.bfloat16) for piece in parts], axis=1)
            fix = jnp.exp2((olds[u] - new) * scale)
            pv = jnp.dot(p, vaug, preferred_element_type=jnp.float32)
            m_s[rows, :] = new
            acc_s[rows, 0:HD] = acc_s[rows, 0:HD] * fix + pv[:, 0:HD]
            acc_s[rows, HD:] = acc_s[rows, HD:] * fix + pv[:, HD:]

    def pair(chip, tiles):
        len0 = len_ref[s * nb + chip * 2]
        len1 = len_ref[s * nb + chip * 2 + 1]

        def valid(g):
            lo, hi = g * 128, g * 128 + 128
            if all(c % cap < low for c in range(lo, hi)):
                return None
            col = lo + lax.broadcasted_iota(jnp.int32, (1, 128), 1)
            return col < jnp.where(col < cap, len0, cap + len1)

        online(tiles, held[chip, :, HD:], valid)

    def pair_all(chip, after=lambda j: None):
        keys_t[:, 0:2 * cap] = held[chip, :, 0:HD].T

        @pl.loop(0, 2)
        def _(j):
            pair(chip, [j * half + row for row in range(0, half, tile)])
            after(j)

    def new_all():
        def mask_for(g):
            col = g * 128 + lax.broadcasted_iota(jnp.int32, (1, 128), 1)
            pos = (col // part) * toks + s * part + col % part
            tok = b * toks + lax.broadcasted_iota(jnp.int32, (tile, 1), 0) % toks
            return pos <= tok

        keys_t[:, 0:nb * part] = news[s].reshape(nb * part, 2 * HD)[:, 0:HD].T

        @pl.loop(0, 2)
        def _(j):
            rows = news[s].reshape(nb * part, 2 * HD)
            online([j * half + row for row in range(0, half, tile)], rows[:, HD:], mask_for)

    def nth_chip(i):
        short = jnp.minimum(z, nc - 1 - z)
        far = i - short
        both = jnp.where(i % 2 == 1, z - (i + 1) // 2, z + (i + 1) // 2)
        single = jnp.where(2 * z < nc, z + far, z - far)
        return jnp.where(i <= 2 * short, both, single)

    def arrive(k):
        @pl.when(z - k >= 0)
        def _():
            copy_c(z - k, core, 1, b).wait_recv()

            @pl.when(z < nc - 1)
            def _():
                copy_c(z - k, core, 1, b + 2).start()
            copy_c(z - k, core, 2, sib).start()

        @pl.when(z + k < nc)
        def _():
            copy_c(z + k, core, 0, b).wait_recv()

            @pl.when(z > 0)
            def _():
                copy_c(z + k, core, 0, b - 2).start()
            copy_c(z + k, core, 2, sib).start()

    for copy in q_in:
        copy.wait()
    copy_c(z, 1 - core, 2, sib).wait_recv()
    pair_all(z)
    arrive(1)
    for d in range(1, nc):
        arrived_n((b + 2 * d) % nb)
        copy_f(d).start()
    for d in range(nc):
        arrived_n((sib + 2 * d) % nb)
    for d in range(1, ns):
        copy_x(d).start()
    new_all()

    def write_pages():
        for d in range(1, ns):
            src = (s + d) % ns
            pltpu.make_async_remote_copy(
                src_ref=news.at[src], dst_ref=news.at[src],
                send_sem=send_x.at[d], recv_sem=recv_x.at[src],
                device_id=(src, b), device_id_type=MESH).wait_recv()
        pages = owner_ref.shape[1]
        total_rows = pages * PAGE
        owned = jnp.where(owner_ref[...] == me, 1.0, 0.0)
        count = jnp.sum(owned, axis=1, keepdims=True)
        owned_b = jnp.broadcast_to(owned, (16, pages))
        up = lax.broadcasted_iota(jnp.int32, (pages, pages), 0)
        across = lax.broadcasted_iota(jnp.int32, (pages, pages), 1)
        earlier = jnp.dot(owned_b.astype(jnp.bfloat16), jnp.where(up < across, 1.0, 0.0).astype(jnp.bfloat16),
                          preferred_element_type=jnp.float32)
        place = jnp.where(owned_b > 0.5, earlier, 128.0).astype(jnp.bfloat16)

        def row_at(shape, axis):
            i = lax.broadcasted_iota(jnp.int32, shape, axis)
            group = i // (nb * part)
            rest = i % (nb * part)
            return (rest // part) * toks + group * part + rest % part

        spread = (row_at((pages, total_rows), 1) // PAGE
                  == lax.broadcasted_iota(jnp.int32, (pages, total_rows), 0))
        placed = jnp.dot(place, jnp.where(spread, 1.0, 0.0).astype(jnp.bfloat16),
                         preferred_element_type=jnp.float32)
        filled = len_ref[me].astype(jnp.float32)
        dest = filled + placed[0:1, :] * PAGE + (row_at((1, total_rows), 1) % PAGE).astype(jnp.float32)
        tail = slots - low
        slot = (low + lax.broadcasted_iota(jnp.int32, (tail, 1), 0)).astype(jnp.float32)
        hot = jnp.where(slot == dest, 1.0, 0.0).astype(jnp.bfloat16)
        rows = news[...].reshape(total_rows, 2 * HD)
        picked = jnp.dot(hot, rows, preferred_element_type=jnp.float32)
        is_new = (slot >= filled) & (slot < filled + PAGE * count)
        tail_in.wait()
        cout_ref[0:low, :] = cache_v[0:low, :]
        cout_ref[low:, :] = jnp.where(is_new, picked, cache_v[low:, :].astype(jnp.float32)).astype(jnp.bfloat16)

    @pl.loop(1, nc - 1)
    def _(i):
        chip = nth_chip(i)
        copy_c(chip, 1 - core, 2, sib).wait_recv()

        inner = (z > 0) & (z < nc - 1)

        def after(j):
            @pl.when((j == 0) & inner)
            def _():
                arrive(i + 1)
        pair_all(chip, after)

        @pl.when(i == nc - 2)
        def _():
            write_pages()

        @pl.when(jnp.logical_not(inner))
        def _():
            arrive(i + 1)

    def copy_o(j, d):
        return pltpu.make_async_remote_copy(
            src_ref=osend.at[j], dst_ref=orecv.at[s],
            send_sem=send_o.at[d], recv_sem=recv_o.at[s],
            device_id=(j, b), device_id_type=MESH)

    def copy_l(j, d):
        return pltpu.make_async_remote_copy(
            src_ref=lsend.at[j], dst_ref=lrecv.at[s],
            send_sem=send_l.at[d], recv_sem=recv_l.at[s],
            device_id=(j, b), device_id_type=MESH)

    last = nth_chip(nc - 1)
    copy_c(last, 1 - core, 2, sib).wait_recv()
    keys_t[:, 0:2 * cap] = held[last, :, 0:HD].T
    eye = (lax.broadcasted_iota(jnp.int32, (toks, toks), 0)
           == lax.broadcasted_iota(jnp.int32, (toks, toks), 1))

    @pl.loop(1, ns + 1)
    def _(d):
        j = (s + d) % ns
        pair(last, [j * rows_t + row for row in range(0, rows_t, tile)])
        for h in range(hpd):
            rows = pl.ds(pl.multiple_of(j * rows_t + h * toks, toks), toks)
            total = acc_s[rows, HD:]
            osend[j, h * toks:(h + 1) * toks, :] = (acc_s[rows, 0:HD] / total).astype(jnp.bfloat16)
            lse = m_s[rows, :] * scale + jnp.log2(total)
            lsend[j, h:h + 1, :] = jnp.sum(jnp.where(eye, lse, 0.0), axis=0, keepdims=True)

        @pl.when(d < ns)
        def _():
            copy_o(j, d).start()
            copy_l(j, d).start()

    orecv[s, :, :] = osend[s, :, :]
    lrecv[s, :, :] = lsend[s, :, :]
    for d in range(1, ns):
        src = (s + d) % ns
        pltpu.make_async_remote_copy(
            src_ref=osend.at[src], dst_ref=orecv.at[src],
            send_sem=send_o.at[d], recv_sem=recv_o.at[src],
            device_id=(src, b), device_id_type=MESH).wait_recv()
        pltpu.make_async_remote_copy(
            src_ref=lsend.at[src], dst_ref=lrecv.at[src],
            send_sem=send_l.at[d], recv_sem=recv_l.at[src],
            device_id=(src, b), device_id_type=MESH).wait_recv()
    for h in range(hpd):
        lses = [lrecv[g, h:h + 1, :] for g in range(ns)]
        top = functools.reduce(jnp.maximum, lses)
        shares = [jnp.exp2(v - top) for v in lses]
        whole = functools.reduce(jnp.add, shares)
        out = jnp.zeros((toks, HD), jnp.float32)
        for g in range(ns):
            share = jnp.broadcast_to(shares[g] / whole, (HD, toks)).T
            out = out + share * orecv[g, h * toks:(h + 1) * toks, :].astype(jnp.float32)
        attn_ref[:, h * HD:(h + 1) * HD] = out.astype(jnp.bfloat16)

    copy_f(0).wait_send()
    for d in range(1, nc):
        copy_n(d).wait_send()
        copy_f(d).wait_send()
    for d in range(1, ns):
        copy_x(d).wait_send()
        copy_o((s + d) % ns, d).wait_send()
        copy_l((s + d) % ns, d).wait_send()

    @pl.loop(0, nc)
    def _(k):
        copy_c(k, core, 2, sib).wait_send()

        @pl.when((k <= z) & (z < nc - 1))
        def _():
            copy_c(k, core, 1, b + 2).wait_send()

        @pl.when((k >= z) & (z > 0))
        def _():
            copy_c(k, core, 0, b - 2).wait_send()


def solution(mesh):
    ns, nb = mesh.shape["seg"], mesh.shape["blk"]
    nc = nb // 2

    def on_device(queries, new_kv, cache_kv, cache_len, page_owner):
        toks = queries.shape[0]
        heads = queries.shape[1] // HD
        slots, width = cache_kv.shape
        pages = page_owner.shape[0]
        cap = slots - PAGE * 4 * pages // (ns * nb)
        low = slots // 2
        rows_t = heads // ns * toks
        tile = min(256, rows_t)
        part = toks // ns
        vmem = pl.BlockSpec(memory_space=pltpu.VMEM)
        hbm = pl.BlockSpec(memory_space=pltpu.HBM)
        dma = pltpu.SemaphoreType.DMA
        return pl.pallas_call(
            functools.partial(body, ns, nb, cap, low, tile),
            out_shape=(jax.ShapeDtypeStruct((toks, heads // ns * HD), jnp.bfloat16),
                       jax.ShapeDtypeStruct((slots, width), jnp.bfloat16)),
            in_specs=[pl.BlockSpec(memory_space=pltpu.SMEM), hbm, hbm, hbm, vmem],
            out_specs=(vmem, vmem),
            scratch_shapes=[
                pltpu.VMEM((nc, 2 * cap, width), jnp.bfloat16),
                pltpu.VMEM((ns, nb, part, width), jnp.bfloat16),
                pltpu.VMEM((slots, width), jnp.bfloat16),
                pltpu.VMEM((HD, max(2 * cap, nb * part)), jnp.bfloat16),
                pltpu.VMEM((heads * toks, HD), jnp.bfloat16),
                pltpu.VMEM((heads * toks, 128), jnp.float32),
                pltpu.VMEM((heads * toks, 2 * HD), jnp.float32),
                pltpu.VMEM((ns, rows_t, HD), jnp.bfloat16),
                pltpu.VMEM((ns, 8, toks), jnp.float32),
                pltpu.VMEM((ns, rows_t, HD), jnp.bfloat16),
                pltpu.VMEM((ns, 8, toks), jnp.float32),
                dma((nc, 3)), dma((nc, 2)),
                dma((nb,)), dma((nb,)),
                dma((ns,)), dma((ns,)),
                dma((ns,)), dma((ns,)),
                dma((ns,)), dma((ns,)), dma((3 + heads,)),
            ],
            compiler_params=pltpu.CompilerParams(
                collective_id=0, has_side_effects=True, vmem_limit_bytes=63 * 1024 * 1024),
            cost_estimate=pl.CostEstimate(
                flops=heads * toks * nb * slots * HD * 4, bytes_accessed=2 * slots * width * 2,
                transcendentals=heads * toks * nb * slots),
        )(cache_len, queries, new_kv, cache_kv, page_owner.reshape(1, pages))

    placed = (P("blk", None), P("blk", None), P(("seg", "blk"), None), P(), P())
    return jax.shard_map(
        on_device,
        mesh=mesh,
        in_specs=placed,
        out_specs=(P("blk", "seg"), P(("seg", "blk"), None)),
        check_vma=False,
    )
```

```python
import functools
import math

import jax
import jax.numpy as jnp
from jax import lax
from jax.experimental import pallas as pl
from jax.experimental.pallas import tpu as pltpu
from jax.sharding import PartitionSpec as P

PAGE = 8
HD = 128
NEG = -1e30
MESH = pl.DeviceIdType.MESH


def body(ns, nb, cap, low, tile, len_ref, q_ref, new_ref, cache_ref, owner_ref, attn_ref, cout_ref,
         held, news, cache_v, keys_t, q_s, m_s, acc_s, osend, lsend, orecv, lrecv,
         send_c, recv_c, send_n, recv_n, send_x, recv_x, send_o, recv_o, send_l, recv_l, in_sem):
    s = lax.axis_index("seg")
    b = lax.axis_index("blk")
    nc = nb // 2
    z = b // 2
    core = b % 2
    sib = z * 2 + 1 - core
    me = s * nb + b
    toks = q_ref.shape[0]
    heads = q_ref.shape[1] // HD
    part_rows = pl.ds(pl.multiple_of(s * (toks // ns), 16), toks // ns)
    hpd = heads // ns
    rows_t = hpd * toks
    half = heads * toks // 2
    part = toks // ns
    slots = cache_ref.shape[0]
    scale = math.log2(math.e) / math.sqrt(HD)

    def shard(chip, c):
        return held.at[chip, pl.ds(pl.multiple_of(c * cap, 16), cap)]

    barrier = pltpu.get_barrier_semaphore()
    for d in range(1, nc):
        pl.semaphore_signal(barrier, inc=1, device_id=(s, (b + 2 * d) % nb), device_id_type=MESH)
    pl.semaphore_signal(barrier, inc=1, device_id=(s, sib), device_id_type=MESH)
    for d in range(1, ns):
        pl.semaphore_signal(barrier, inc=1, device_id=((s + d) % ns, b), device_id_type=MESH)
    own_in = pltpu.make_async_copy(cache_ref.at[pl.ds(0, cap)], shard(z, core), in_sem.at[0])
    new_in = pltpu.make_async_copy(new_ref.at[part_rows], news.at[s, b], in_sem.at[1])
    tail_in = pltpu.make_async_copy(cache_ref, cache_v, in_sem.at[2])
    q_in = [pltpu.make_async_copy(q_ref.at[:, pl.ds(h * HD, HD)], q_s.at[pl.ds(h * toks, toks)], in_sem.at[3 + h])
            for h in range(heads)]
    own_in.start()
    new_in.start()
    for copy in q_in:
        copy.start()
    tail_in.start()
    own_in.wait()
    new_in.wait()
    pl.semaphore_wait(barrier, nc + ns - 1)

    def copy_c(chip, c, way, target):
        return pltpu.make_async_remote_copy(
            src_ref=shard(chip, c), dst_ref=shard(chip, c),
            send_sem=send_c.at[chip, way], recv_sem=recv_c.at[chip, c],
            device_id=(s, target), device_id_type=MESH)

    def copy_n(d):
        return pltpu.make_async_remote_copy(
            src_ref=news.at[s, b], dst_ref=news.at[s, b],
            send_sem=send_n.at[d], recv_sem=recv_n.at[b],
            device_id=(s, (b + 2 * d) % nb), device_id_type=MESH)

    def copy_f(d):
        src = (b + 2 * d) % nb
        return pltpu.make_async_remote_copy(
            src_ref=news.at[s, src], dst_ref=news.at[s, src],
            send_sem=send_n.at[nc + d], recv_sem=recv_n.at[src],
            device_id=(s, sib), device_id_type=MESH)

    def arrived_n(src):
        pltpu.make_async_remote_copy(
            src_ref=news.at[s, src], dst_ref=news.at[s, src],
            send_sem=send_n.at[0], recv_sem=recv_n.at[src],
            device_id=(s, sib), device_id_type=MESH).wait_recv()

    def copy_x(d):
        return pltpu.make_async_remote_copy(
            src_ref=news.at[s], dst_ref=news.at[s],
            send_sem=send_x.at[d], recv_sem=recv_x.at[s],
            device_id=((s + d) % ns, b), device_id_type=MESH)

    @pl.when(z > 0)
    def _():
        copy_c(z, core, 0, b - 2).start()

    @pl.when(z < nc - 1)
    def _():
        copy_c(z, core, 1, b + 2).start()

    copy_c(z, core, 2, sib).start()
    copy_f(0).start()
    for d in range(1, nc):
        copy_n(d).start()

    m_s[...] = jnp.full_like(m_s, NEG)
    acc_s[...] = jnp.zeros_like(acc_s)

    def online(tiles, vals, valid):
        tiles = [pl.ds(pl.multiple_of(row, tile), tile) for row in tiles]
        n = vals.shape[0]
        olds = [m_s[rows, :] for rows in tiles]
        vaug = jnp.concatenate([vals, jnp.ones_like(vals)], axis=1)

        def score(rows):
            return jnp.dot(q_s[rows, :], keys_t[:, 0:n], preferred_element_type=jnp.float32)

        ahead = score(tiles[0])
        for u, rows in enumerate(tiles):
            sc = ahead
            if u + 1 < len(tiles):
                ahead = score(tiles[u + 1])
            parts = []
            for g in range(n // 128):
                piece = sc[:, g * 128:(g + 1) * 128]
                mask = valid(g)
                parts.append(piece if mask is None else jnp.where(mask, piece, NEG))
            top = functools.reduce(jnp.maximum, parts)
            new = jnp.maximum(olds[u], jnp.max(top, axis=1, keepdims=True))
            p = jnp.concatenate(
                [jnp.exp2(((piece - new) * scale).astype(jnp.bfloat16)) for piece in parts], axis=1)
            fix = jnp.exp2((olds[u] - new) * scale)
            pv = jnp.dot(p, vaug, preferred_element_type=jnp.float32)
            m_s[rows, :] = new
            acc_s[rows, 0:HD] = acc_s[rows, 0:HD] * fix + pv[:, 0:HD]
            acc_s[rows, HD:] = acc_s[rows, HD:] * fix + pv[:, HD:]

    def pair(chip, tiles):
        len0 = len_ref[s * nb + chip * 2]
        len1 = len_ref[s * nb + chip * 2 + 1]

        def valid(g):
            lo, hi = g * 128, g * 128 + 128
            if all(c % cap < low for c in range(lo, hi)):
                return None
            col = lo + lax.broadcasted_iota(jnp.int32, (1, 128), 1)
            return col < jnp.where(col < cap, len0, cap + len1)

        online(tiles, held[chip, :, HD:], valid)

    def pair_all(chip, after=lambda j: None):
        keys_t[:, 0:2 * cap] = held[chip, :, 0:HD].T

        @pl.loop(0, 2)
        def _(j):
            pair(chip, [j * half + row for row in range(0, half, tile)])
            after(j)

    def new_all():
        def mask_for(g):
            col = g * 128 + lax.broadcasted_iota(jnp.int32, (1, 128), 1)
            pos = (col // part) * toks + s * part + col % part
            tok = b * toks + lax.broadcasted_iota(jnp.int32, (tile, 1), 0) % toks
            return pos <= tok

        keys_t[:, 0:nb * part] = news[s].reshape(nb * part, 2 * HD)[:, 0:HD].T

        @pl.loop(0, 2)
        def _(j):
            rows = news[s].reshape(nb * part, 2 * HD)
            online([j * half + row for row in range(0, half, tile)], rows[:, HD:], mask_for)

    def nth_chip(i):
        short = jnp.minimum(z, nc - 1 - z)
        far = i - short
        both = jnp.where(i % 2 == 1, z - (i + 1) // 2, z + (i + 1) // 2)
        single = jnp.where(2 * z < nc, z + far, z - far)
        return jnp.where(i <= 2 * short, both, single)

    def arrive(k):
        @pl.when(z - k >= 0)
        def _():
            copy_c(z - k, core, 1, b).wait_recv()

            @pl.when(z < nc - 1)
            def _():
                copy_c(z - k, core, 1, b + 2).start()
            copy_c(z - k, core, 2, sib).start()

        @pl.when(z + k < nc)
        def _():
            copy_c(z + k, core, 0, b).wait_recv()

            @pl.when(z > 0)
            def _():
                copy_c(z + k, core, 0, b - 2).start()
            copy_c(z + k, core, 2, sib).start()

    for copy in q_in:
        copy.wait()
    copy_c(z, 1 - core, 2, sib).wait_recv()
    pair_all(z)
    arrive(1)
    for d in range(1, nc):
        arrived_n((b + 2 * d) % nb)
        copy_f(d).start()
    for d in range(nc):
        arrived_n((sib + 2 * d) % nb)
    for d in range(1, ns):
        copy_x(d).start()
    new_all()

    @pl.loop(1, nc - 1)
    def _(i):
        chip = nth_chip(i)
        copy_c(chip, 1 - core, 2, sib).wait_recv()

        def after(j):
            @pl.when(j == jnp.where((z > 0) & (z < nc - 1), 0, 1))
            def _():
                arrive(i + 1)
        pair_all(chip, after)

    def copy_o(j, d):
        return pltpu.make_async_remote_copy(
            src_ref=osend.at[j], dst_ref=orecv.at[s],
            send_sem=send_o.at[d], recv_sem=recv_o.at[s],
            device_id=(j, b), device_id_type=MESH)

    def copy_l(j, d):
        return pltpu.make_async_remote_copy(
            src_ref=lsend.at[j], dst_ref=lrecv.at[s],
            send_sem=send_l.at[d], recv_sem=recv_l.at[s],
            device_id=(j, b), device_id_type=MESH)

    last = nth_chip(nc - 1)
    copy_c(last, 1 - core, 2, sib).wait_recv()
    keys_t[:, 0:2 * cap] = held[last, :, 0:HD].T
    eye = (lax.broadcasted_iota(jnp.int32, (toks, toks), 0)
           == lax.broadcasted_iota(jnp.int32, (toks, toks), 1))

    @pl.loop(1, ns + 1)
    def _(d):
        j = (s + d) % ns
        pair(last, [j * rows_t + row for row in range(0, rows_t, tile)])
        for h in range(hpd):
            rows = pl.ds(pl.multiple_of(j * rows_t + h * toks, toks), toks)
            total = acc_s[rows, HD:]
            osend[j, h * toks:(h + 1) * toks, :] = (acc_s[rows, 0:HD] / total).astype(jnp.bfloat16)
            lse = m_s[rows, :] * scale + jnp.log2(total)
            lsend[j, h:h + 1, :] = jnp.sum(jnp.where(eye, lse, 0.0), axis=0, keepdims=True)

        @pl.when(d < ns)
        def _():
            copy_o(j, d).start()
            copy_l(j, d).start()

    for d in range(1, ns):
        src = (s + d) % ns
        pltpu.make_async_remote_copy(
            src_ref=news.at[src], dst_ref=news.at[src],
            send_sem=send_x.at[d], recv_sem=recv_x.at[src],
            device_id=(src, b), device_id_type=MESH).wait_recv()
    pages = owner_ref.shape[1]
    total_rows = pages * PAGE
    owned = jnp.where(owner_ref[...] == me, 1.0, 0.0)
    count = jnp.sum(owned, axis=1, keepdims=True)
    owned_b = jnp.broadcast_to(owned, (16, pages))
    up = lax.broadcasted_iota(jnp.int32, (pages, pages), 0)
    across = lax.broadcasted_iota(jnp.int32, (pages, pages), 1)
    earlier = jnp.dot(owned_b.astype(jnp.bfloat16), jnp.where(up < across, 1.0, 0.0).astype(jnp.bfloat16),
                      preferred_element_type=jnp.float32)
    place = jnp.where(owned_b > 0.5, earlier, 128.0).astype(jnp.bfloat16)

    def row_at(shape, axis):
        i = lax.broadcasted_iota(jnp.int32, shape, axis)
        group = i // (nb * part)
        rest = i % (nb * part)
        return (rest // part) * toks + group * part + rest % part

    spread = (row_at((pages, total_rows), 1) // PAGE
              == lax.broadcasted_iota(jnp.int32, (pages, total_rows), 0))
    placed = jnp.dot(place, jnp.where(spread, 1.0, 0.0).astype(jnp.bfloat16),
                     preferred_element_type=jnp.float32)
    filled = len_ref[me].astype(jnp.float32)
    dest = filled + placed[0:1, :] * PAGE + (row_at((1, total_rows), 1) % PAGE).astype(jnp.float32)
    tail = slots - low
    slot = (low + lax.broadcasted_iota(jnp.int32, (tail, 1), 0)).astype(jnp.float32)
    hot = jnp.where(slot == dest, 1.0, 0.0).astype(jnp.bfloat16)
    rows = news[...].reshape(total_rows, 2 * HD)
    picked = jnp.dot(hot, rows, preferred_element_type=jnp.float32)
    is_new = (slot >= filled) & (slot < filled + PAGE * count)
    tail_in.wait()
    cout_ref[0:low, :] = cache_v[0:low, :]
    cout_ref[low:, :] = jnp.where(is_new, picked, cache_v[low:, :].astype(jnp.float32)).astype(jnp.bfloat16)

    orecv[s, :, :] = osend[s, :, :]
    lrecv[s, :, :] = lsend[s, :, :]
    for d in range(1, ns):
        src = (s + d) % ns
        pltpu.make_async_remote_copy(
            src_ref=osend.at[src], dst_ref=orecv.at[src],
            send_sem=send_o.at[d], recv_sem=recv_o.at[src],
            device_id=(src, b), device_id_type=MESH).wait_recv()
        pltpu.make_async_remote_copy(
            src_ref=lsend.at[src], dst_ref=lrecv.at[src],
            send_sem=send_l.at[d], recv_sem=recv_l.at[src],
            device_id=(src, b), device_id_type=MESH).wait_recv()
    for h in range(hpd):
        lses = [lrecv[g, h:h + 1, :] for g in range(ns)]
        top = functools.reduce(jnp.maximum, lses)
        shares = [jnp.exp2(v - top) for v in lses]
        whole = functools.reduce(jnp.add, shares)
        out = jnp.zeros((toks, HD), jnp.float32)
        for g in range(ns):
            share = jnp.broadcast_to(shares[g] / whole, (HD, toks)).T
            out = out + share * orecv[g, h * toks:(h + 1) * toks, :].astype(jnp.float32)
        attn_ref[:, h * HD:(h + 1) * HD] = out.astype(jnp.bfloat16)

    copy_f(0).wait_send()
    for d in range(1, nc):
        copy_n(d).wait_send()
        copy_f(d).wait_send()
    for d in range(1, ns):
        copy_x(d).wait_send()
        copy_o((s + d) % ns, d).wait_send()
        copy_l((s + d) % ns, d).wait_send()

    @pl.loop(0, nc)
    def _(k):
        copy_c(k, core, 2, sib).wait_send()

        @pl.when((k <= z) & (z < nc - 1))
        def _():
            copy_c(k, core, 1, b + 2).wait_send()

        @pl.when((k >= z) & (z > 0))
        def _():
            copy_c(k, core, 0, b - 2).wait_send()


def solution(mesh):
    ns, nb = mesh.shape["seg"], mesh.shape["blk"]
    nc = nb // 2

    def on_device(queries, new_kv, cache_kv, cache_len, page_owner):
        toks = queries.shape[0]
        heads = queries.shape[1] // HD
        slots, width = cache_kv.shape
        pages = page_owner.shape[0]
        cap = slots - PAGE * 4 * pages // (ns * nb)
        low = slots // 2
        rows_t = heads // ns * toks
        tile = min(256, rows_t)
        part = toks // ns
        vmem = pl.BlockSpec(memory_space=pltpu.VMEM)
        hbm = pl.BlockSpec(memory_space=pltpu.HBM)
        dma = pltpu.SemaphoreType.DMA
        return pl.pallas_call(
            functools.partial(body, ns, nb, cap, low, tile),
            out_shape=(jax.ShapeDtypeStruct((toks, heads // ns * HD), jnp.bfloat16),
                       jax.ShapeDtypeStruct((slots, width), jnp.bfloat16)),
            in_specs=[pl.BlockSpec(memory_space=pltpu.SMEM), hbm, hbm, hbm, vmem],
            out_specs=(vmem, vmem),
            scratch_shapes=[
                pltpu.VMEM((nc, 2 * cap, width), jnp.bfloat16),
                pltpu.VMEM((ns, nb, part, width), jnp.bfloat16),
                pltpu.VMEM((slots, width), jnp.bfloat16),
                pltpu.VMEM((HD, max(2 * cap, nb * part)), jnp.bfloat16),
                pltpu.VMEM((heads * toks, HD), jnp.bfloat16),
                pltpu.VMEM((heads * toks, 128), jnp.float32),
                pltpu.VMEM((heads * toks, 2 * HD), jnp.float32),
                pltpu.VMEM((ns, rows_t, HD), jnp.bfloat16),
                pltpu.VMEM((ns, 8, toks), jnp.float32),
                pltpu.VMEM((ns, rows_t, HD), jnp.bfloat16),
                pltpu.VMEM((ns, 8, toks), jnp.float32),
                dma((nc, 3)), dma((nc, 2)),
                dma((nb,)), dma((nb,)),
                dma((ns,)), dma((ns,)),
                dma((ns,)), dma((ns,)),
                dma((ns,)), dma((ns,)), dma((3 + heads,)),
            ],
            compiler_params=pltpu.CompilerParams(
                collective_id=0, has_side_effects=True, vmem_limit_bytes=63 * 1024 * 1024),
            cost_estimate=pl.CostEstimate(
                flops=heads * toks * nb * slots * HD * 4, bytes_accessed=2 * slots * width * 2,
                transcendentals=heads * toks * nb * slots),
        )(cache_len, queries, new_kv, cache_kv, page_owner.reshape(1, pages))

    placed = (P("blk", None), P("blk", None), P(("seg", "blk"), None), P(), P())
    return jax.shard_map(
        on_device,
        mesh=mesh,
        in_specs=placed,
        out_specs=(P("blk", "seg"), P(("seg", "blk"), None)),
        check_vma=False,
    )
```
